256 devices in a mesh: occ: 16 (over y, z_lo), aux: 16 (over z_hi, x, core).
Axes of the slice: x: 4, y: 4, z: 8 (z_hi: 2, z_lo: 4; z = z_hi * 4 + z_lo), core: 2. Of those that a mesh axis runs over, the one named last changes fastest.
Arguments:
- three_index: bfloat16 [6144, 32, 1536], P(('occ', 'aux')), may hold values from -0.099609375 to 0.099609375
- occupied_energy: float32 [32], replicated, may hold values from -1.5 to -0.3
- virtual_energy: float32 [1536], replicated, may hold values from 0.2 to 4
- pair_list: int32 [16, 2], P('occ'), may hold values from 0 to 31, as said below
Outputs:
- density: float32 [1536, 1536], P('aux', 'occ')
The draws below stay inside these ranges and needn't reach their ends.
Inputs may be any that keep to these rules, and one draw needn't show every extreme that they name: `pair_list`: row o + r is the pair handled by occupied block o in round r: its first index lies in o * 2 to o * 2 + 1, and in each round r the second indices of all 16 rows of that round lie in one common block of 2 consecutive orbitals starting at a multiple of 2.
All inputs are finite; a program needn't handle non-finite values.
Results may differ from the reference program's by a relative error of at most 0.0003.
Values may be sent and summed in bfloat16 or wider, within the bound.
A program may use at most 64 MiB of HBM per device.

```python
import math
import jax
import jax.numpy as jnp
from jax import lax

NAUX = 6144
NVIRT = 1536
OCC_DEV = 2
ROUNDS = 1
NOCC = 32
PAIRS = 16
N_OCC = 16
N_AUX = 16


def draw_pair_list(key, part):
    key = jax.random.fold_in(key, 7)
    key_owner, key_shift, key_pick = jax.random.split(key, 3)
    owners = jax.random.randint(key_owner, (ROUNDS,), 0, N_OCC)
    shifts = jax.random.randint(key_shift, (N_OCC,), 0, OCC_DEV)
    shifts = shifts.at[0].set(0)
    shifts = shifts.at[N_OCC - 1].set(OCC_DEV - 1)
    picks = jax.random.randint(key_pick, (N_OCC, ROUNDS), 0, OCC_DEV)
    groups = jnp.arange(N_OCC, dtype=jnp.int32)[:, None]
    rounds = jnp.arange(ROUNDS, dtype=jnp.int32)[None, :]
    first_index = groups * OCC_DEV + (rounds + shifts[:, None]) % OCC_DEV
    second_index = owners[None, :] * OCC_DEV + picks
    return jnp.stack([first_index, second_index], axis=-1).reshape(PAIRS, 2).astype(jnp.int32)


def block_scale(key, shape, shards, smallest, high):
    level = 1.0
    for dim, shards_of in shards:
        steps = jax.random.uniform(jax.random.fold_in(jax.random.fold_in(key, 6), dim), (shards_of,), jnp.float32, smallest / len(shards), high / len(shards))
        level = level * jnp.repeat(jnp.exp(steps), shape[dim] // shards_of).reshape((-1,) + (1,) * (len(shape) - 1 - dim))
    return level


def gaussian(own_key, dims, deviation, bound, cuts=(), held_as=jnp.bfloat16):
    level = block_scale(own_key, dims, cuts, -0.22, 0.18) if cuts else 1.0
    drawn = jax.random.normal(own_key, dims, jnp.float32) * deviation * level
    return jnp.minimum(jnp.maximum(drawn, -bound), bound).astype(held_as)


def setup_inputs(seed: int = 0) -> dict:
    key_list = jax.random.split(jax.random.key(seed), 5)
    return {
        "three_index": gaussian(key_list[0], (NAUX, NOCC, NVIRT), 0.018, 0.099609375, ((0, 256),)),
        "occupied_energy": jnp.clip(jax.random.uniform(key_list[1], (NOCC,), jnp.float32, -1.5, -0.3), -1.5, -0.3),
        "virtual_energy": jnp.clip(jnp.exp(jax.random.uniform(key_list[2], (NVIRT,), jnp.float32, math.log(0.2), math.log(4.0))), 0.2, 4.0),
        "pair_list": draw_pair_list(jax.random.fold_in(key_list[4], 71), 0),
    }


def reference(three_index, occupied_energy, virtual_energy, pair_list):
    group_depth = NAUX // (N_OCC * N_AUX)

    def one_pair(running_sum, pair_row):
        orbital_one = lax.dynamic_index_in_dim(three_index, pair_row[0], 1, keepdims=False)
        orbital_two = lax.dynamic_index_in_dim(three_index, pair_row[1], 1, keepdims=False)
        orbital_one = orbital_one.astype(jnp.float32).reshape(N_OCC, N_AUX, group_depth, NVIRT)
        orbital_two = orbital_two.astype(jnp.float32).reshape(N_OCC, N_AUX, group_depth, NVIRT)
        group_parts = jnp.einsum("kgma,kgmb->gab", orbital_one, orbital_two, precision=lax.Precision.HIGHEST)
        coulomb = jnp.sum(group_parts, axis=0)
        shift_energy = occupied_energy[pair_row[0]] + occupied_energy[pair_row[1]]
        denominator = virtual_energy[:, None] + virtual_energy[None, :] - shift_energy
        amplitudes = -coulomb / denominator
        added = lax.dot_general(amplitudes, amplitudes, (((1,), (1,)), ((), ())), precision=lax.Precision.HIGHEST, preferred_element_type=jnp.float32)
        return running_sum + added, None

    start_sum = jnp.zeros((NVIRT, NVIRT), jnp.float32)
    density, _ = lax.scan(one_pair, start_sum, pair_list)
    return density
```

```python
import functools

import jax
import jax.numpy as jnp
from jax import lax
from jax.experimental import pallas as pl
from jax.experimental.pallas import tpu as pltpu
from jax.sharding import PartitionSpec as P

MESH = pl.DeviceIdType.MESH
F32 = jnp.float32
BF16 = jnp.bfloat16
I16 = jnp.int16
NX, NY, NZ = 4, 4, 8
PLANE = NX * NY
CODE = 16


def position():
    occ, aux = lax.axis_index("occ"), lax.axis_index("aux")
    core = lax.rem(aux, 2)
    x = lax.rem(lax.div(aux, 2), NX)
    z = lax.div(aux, 2 * NX) * 4 + lax.rem(occ, 4)
    return x, lax.div(occ, 4), z, core


def device(x, y, z, core):
    return (y * 4 + lax.rem(z, 4), (lax.div(z, 4) * NX + x) * 2 + core)


def greet(peers_of, count, others):
    barrier = pltpu.get_barrier_semaphore()

    def signal(k, carry):
        pl.semaphore_signal(barrier, inc=1, device_id=peers_of(k), device_id_type=MESH)
        return carry

    lax.fori_loop(1, count, signal, 0)
    for other in others:
        pl.semaphore_signal(barrier, inc=1, device_id=other, device_id_type=MESH)
    pl.semaphore_wait(barrier, count - 1 + len(others))


def remote(src, dst, send, recv, dev):
    return pltpu.make_async_remote_copy(
        src_ref=src, dst_ref=dst, send_sem=send, recv_sem=recv, device_id=dev, device_id_type=MESH
    )


def exchange_kernel(half, three, pairs, sibling_rows, listed, mine, table, send, recv, half_send, half_recv):
    occ, aux = lax.axis_index("occ"), lax.axis_index("aux")
    x, y, z, core = position()
    sibling = device(x, y, z, 1 - core)

    def peer(k):
        return (lax.rem(occ + k, 16), aux)

    mine[...] = jnp.zeros_like(mine)
    mine[0:1, 0:2] = pairs[...]
    greet(peer, 16, [sibling])
    columns = pl.ds(pl.multiple_of((1 - core) * half, 128), half)
    rows = remote(three.at[:, :, columns], sibling_rows, half_send, half_recv, sibling)

    def copy(k):
        return remote(mine, table.at[occ], send.at[k], recv.at[k], peer(k))

    def start(k, carry):
        copy(k).start()
        return carry

    lax.fori_loop(1, 16, start, 0)
    rows.start()
    table[occ] = mine[...]

    def finish(k, carry):
        copy(k).wait_send()
        came = lax.rem(occ + 16 - k, 16)
        remote(mine, table.at[came], send.at[k], recv.at[k], peer(k)).wait_recv()
        return carry

    lax.fori_loop(1, 16, finish, 0)
    listed[...] = table[...]
    rows.wait()


def exchange(three, pairs, half):
    depth, orbitals, _ = three.shape
    return pl.pallas_call(
        functools.partial(exchange_kernel, half),
        out_shape=(
            jax.ShapeDtypeStruct((depth, orbitals, half), BF16),
            jax.ShapeDtypeStruct((16, 8, 128), jnp.int32),
        ),
        in_specs=[pl.BlockSpec(memory_space=pl.ANY), pl.BlockSpec(memory_space=pltpu.VMEM)],
        out_specs=(pl.BlockSpec(memory_space=pl.ANY), pl.BlockSpec(memory_space=pltpu.VMEM)),
        scratch_shapes=[
            pltpu.VMEM((8, 128), jnp.int32),
            pltpu.VMEM((16, 8, 128), jnp.int32),
            pltpu.SemaphoreType.DMA((16,)),
            pltpu.SemaphoreType.DMA((16,)),
            pltpu.SemaphoreType.DMA,
            pltpu.SemaphoreType.DMA,
        ],
        compiler_params=pltpu.CompilerParams(collective_id=0, has_side_effects=True),
        name="exchange",
    )(three, pairs)


def encode(block, ref):
    rows = block.shape[0]
    top = jnp.maximum(jnp.max(jnp.abs(block), axis=0, keepdims=True), 1e-30)
    level = jnp.ceil(jnp.log(top) * 64.0)
    ref[0:rows, :] = jnp.round(block * (32000.0 * jnp.exp(level * (-1.0 / 64.0)))).astype(jnp.int32).astype(I16)
    ref[rows : rows + CODE, :] = jnp.broadcast_to(level, (CODE, block.shape[1])).astype(jnp.int32).astype(I16)


def decode(ref):
    rows = ref.shape[0] - CODE
    level = ref[rows : rows + CODE, :].astype(jnp.int32).astype(F32)[0:1, :]
    return ref[0:rows, :].astype(jnp.int32).astype(F32) * (jnp.exp(level * (1.0 / 64.0)) * (1.0 / 32000.0))


def dot_rows(a, b):
    return lax.dot_general(a, b, (((0,), (0,)), ((), ())), preferred_element_type=F32)


def density_kernel(
    half, slab, a_msg, b_msg, eb, ea, out,
    a_in, b_in, b_sib, coulomb, up_out, up_in, down_out, down_in, amp, high, low, left_high, left_low,
    dens, y_up0, y_up1, y_down0, y_down1, part, z_up, z_down,
    own_sem, a_send, a_recv, b_send, b_recv, s_send, s_recv, ring_send, ring_recv, x_send, x_recv, c_send, c_recv,
    y_send, y_recv, z_send, z_recv,
):
    x, y, z, core = position()
    me = x * NY + y
    cut = half // 2
    side = out.shape[0]

    def peer(k):
        to = lax.rem(me + k, PLANE)
        return device(lax.div(to, NY), lax.rem(to, NY), z, core)

    sibling = device(x, y, z, 1 - core)
    z_next, z_prev = lax.rem(z + 1, NZ), lax.rem(z + NZ - 1, NZ)
    above, below = device(x, y, z_next, core), device(x, y, z_prev, core)
    greet(peer, PLANE, [sibling, above, below])

    def to_plane(msg, into, send, recv, k):
        return remote(msg.at[lax.rem(me + k, PLANE)], into.at[me], send.at[k], recv.at[k], peer(k))

    def from_plane(msg, into, send, recv, k):
        came = lax.rem(me + PLANE - k, PLANE)
        return remote(msg.at[came], into.at[came], send.at[k], recv.at[k], peer(k))

    def to_sibling(k):
        came = lax.rem(me + PLANE - k, PLANE)
        return remote(b_in.at[came], b_sib.at[came], s_send.at[k], s_recv.at[k], sibling)

    def start_b(k, carry):
        to_plane(b_msg, b_in, b_send, b_recv, k).start()
        return carry

    def start_a(k, carry):
        to_plane(a_msg, a_in, a_send, a_recv, k).start()
        return carry

    lax.fori_loop(1, PLANE, start_b, 0)
    own_b = pltpu.make_async_copy(b_msg.at[me], b_in.at[me], own_sem.at[0])
    own_a = pltpu.make_async_copy(a_msg.at[me], a_in.at[me], own_sem.at[1])
    own_b.start()
    own_a.start()
    lax.fori_loop(1, PLANE, start_a, 0)
    own_b.wait()
    to_sibling(0).start()

    def pass_on(k, carry):
        from_plane(b_msg, b_in, b_send, b_recv, k).wait_recv()
        to_sibling(k).start()
        return carry

    lax.fori_loop(1, PLANE, pass_on, 0)
    own_a.wait()

    def take(k, carry):
        from_plane(a_msg, a_in, a_send, a_recv, k).wait_recv()
        return carry

    lax.fori_loop(1, PLANE, take, 0)

    def take_sibling(k, carry):
        to_sibling(k).wait_recv()
        return carry

    lax.fori_loop(0, PLANE, take_sibling, 0)

    rows_a = a_in[...].reshape(-1, half)
    tile = 256
    for source, which in ((b_in, core), (b_sib, 1 - core)):
        for n in range(half // tile):
            lhs = source[:, :, n * tile : (n + 1) * tile].reshape(-1, tile)
            coulomb[pl.ds(pl.multiple_of(which * half + n * tile, tile), tile), :] = dot_rows(lhs, rows_a)

    def block(w):
        return coulomb[pl.ds(pl.multiple_of(w * slab, slab), slab), :]

    far = block(lax.rem(z + 4, NZ))
    encode(far[:, :cut], up_out.at[0, :, :cut])
    up = [remote(up_out.at[0, :, :cut], up_in.at[0, :, :cut], ring_send.at[0], ring_recv.at[0], above)]
    up[0].start()
    encode(far[:, cut:], down_out.at[0, :, cut:])
    down = [remote(down_out.at[0, :, cut:], down_in.at[0, :, cut:], ring_send.at[4], ring_recv.at[4], below)]
    down[0].start()
    for t in range(1, 4):
        for way, sent, box, into, w, to in (
            (0, up, up_out, up_in, lax.rem(z + 4 - t, NZ), above),
            (1, down, down_out, down_in, lax.rem(z + 4 + t, NZ), below),
        ):
            sent[t - 1].wait_recv()
            mine = block(w)
            if t == 1:
                columns = slice(cut, half) if way else slice(0, cut)
                rest = slice(0, cut) if way else slice(cut, half)
                encode(mine[:, columns] + decode(into.at[0, :, columns]), box.at[t, :, columns])
                encode(mine[:, rest], box.at[t, :, rest])
            else:
                encode(mine + decode(into.at[t - 1]), box.at[t])
            sent.append(remote(box.at[t], into.at[t], ring_send.at[4 * way + t], ring_recv.at[4 * way + t], to))
            sent[t].start()
    own = block(z)
    up[3].wait_recv()
    down[3].wait_recv()
    own = own + decode(up_in.at[3]) + decode(down_in.at[3])

    encode(-own / (eb[...] + ea[...]), amp.at[core, x])
    x_next, x_prev, x_far = lax.rem(x + 1, NX), lax.rem(x + NX - 1, NX), lax.rem(x + 2, NX)
    right, left = device(x_next, y, z, core), device(x_prev, y, z, core)

    def same_slot(k, columns, n, dev):
        ref = amp.at[core, k] if columns is None else amp.at[core, k, :, columns]
        return remote(ref, ref, x_send.at[n], x_recv.at[n], dev)

    def share(k, n):
        return remote(amp.at[core, k], amp.at[core, k], c_send.at[n], c_recv.at[n], sibling)

    def shared(k, n):
        return remote(amp.at[1 - core, k], amp.at[1 - core, k], c_send.at[n], c_recv.at[n], sibling)

    low_cut, high_cut = slice(0, cut), slice(cut, half)
    sends = [same_slot(x, None, 0, right), same_slot(x, None, 1, left), share(x, 0)]
    for s in sends:
        s.start()
    same_slot(x_prev, None, 0, right).wait_recv()
    sends += [same_slot(x_prev, low_cut, 2, right), share(x_prev, 1)]
    for s in sends[-2:]:
        s.start()
    same_slot(x_next, None, 1, left).wait_recv()
    sends += [same_slot(x_next, high_cut, 3, left), share(x_next, 2)]
    for s in sends[-2:]:
        s.start()
    same_slot(x_far, low_cut, 2, right).wait_recv()
    same_slot(x_far, high_cut, 3, left).wait_recv()
    sends.append(share(x_far, 3))
    sends[-1].start()
    for k, n in ((x, 0), (x_prev, 1), (x_next, 2), (x_far, 3)):
        shared(k, n).wait_recv()

    shift = lax.rem(half - side * (x * 2 + core), half)
    for h in range(2):
        for k in range(NX):
            value = decode(amp.at[h, k])
            rows = slice(k * slab, (k + 1) * slab)
            columns = slice(h * half, (h + 1) * half)
            top = value.astype(BF16)
            high[rows, columns] = top
            low[rows, columns] = (value - top.astype(F32)).astype(BF16)
            turned = pltpu.roll(value, shift, 1)[:, 0:128]
            top = turned.astype(BF16)
            left_high[h, rows, :] = top
            left_low[h, rows, :] = (turned - top.astype(F32)).astype(BF16)
    width = dens.shape[3]
    for h in range(2):
        for n in range(NY):
            columns = slice(n * width, (n + 1) * width)
            total = dot_rows(left_high[h], low[:, columns]) + dot_rows(left_low[h], high[:, columns])
            total = total + dot_rows(left_low[h], low[:, columns])
            dens[n, h] = (total + dot_rows(left_high[h], high[:, columns]))[0:side, :]

    y_next, y_prev, y_far = lax.rem(y + 1, NY), lax.rem(y + NY - 1, NY), lax.rem(y + 2, NY)
    north, south = device(x, y_next, z, core), device(x, y_prev, z, core)
    first = remote(dens.at[y_far, 0], y_up0, y_send.at[0], y_recv.at[0], north)
    second = remote(dens.at[y_far, 1], y_down0, y_send.at[1], y_recv.at[1], south)
    first.start()
    second.start()
    first.wait_recv()
    dens[y_next, 0] = dens[y_next, 0] + y_up0[...]
    third = remote(dens.at[y_next], y_up1, y_send.at[2], y_recv.at[2], north)
    third.start()
    second.wait_recv()
    dens[y_prev, 1] = dens[y_prev, 1] + y_down0[...]
    fourth = remote(dens.at[y_prev], y_down1, y_send.at[3], y_recv.at[3], south)
    fourth.start()
    third.wait_recv()
    fourth.wait_recv()
    for h in range(2):
        total = dens[y, h] + y_up1[h] + y_down1[h]
        for n in range(4):
            part[h * 4 + n] = total[:, n * side : (n + 1) * side]

    far_z = lax.rem(z + 4, NZ)
    mid = side // 2
    up_z = [remote(part.at[far_z, :mid], z_up.at[0, :mid], z_send.at[0], z_recv.at[0], above)]
    down_z = [remote(part.at[far_z, mid:], z_down.at[0, mid:], z_send.at[4], z_recv.at[4], below)]
    up_z[0].start()
    down_z[0].start()
    for t in range(1, 4):
        for way, sent, into, w, to in (
            (0, up_z, z_up, lax.rem(z + 4 - t, NZ), above),
            (1, down_z, z_down, lax.rem(z + 4 + t, NZ), below),
        ):
            sent[t - 1].wait_recv()
            if t > 1:
                part[w] = part[w] + into[t - 1]
            elif way:
                part[w, mid:] = part[w, mid:] + into[0, mid:]
            else:
                part[w, :mid] = part[w, :mid] + into[0, :mid]
            sent.append(remote(part.at[w], into.at[t], z_send.at[4 * way + t], z_recv.at[4 * way + t], to))
            sent[t].start()
    up_z[3].wait_recv()
    down_z[3].wait_recv()
    out[...] = part[z] + z_up[3] + z_down[3]

    def drain(k, carry):
        to_plane(b_msg, b_in, b_send, b_recv, k).wait_send()
        to_plane(a_msg, a_in, a_send, a_recv, k).wait_send()
        return carry

    lax.fori_loop(1, PLANE, drain, 0)

    def drain_sibling(k, carry):
        to_sibling(k).wait_send()
        return carry

    lax.fori_loop(0, PLANE, drain_sibling, 0)
    for s in up + down + sends + [first, second, third, fourth] + up_z + down_z:
        s.wait_send()


def density(a_msg, b_msg, eb, ea):
    _, depth, half = a_msg.shape
    virtual = 2 * half
    slab = virtual // NZ
    side = virtual // 16
    coded = slab + CODE
    dma = pltpu.SemaphoreType.DMA
    vmem = pltpu.VMEM
    return pl.pallas_call(
        functools.partial(density_kernel, half, slab),
        out_shape=jax.ShapeDtypeStruct((side, side), F32),
        in_specs=[pl.BlockSpec(memory_space=pl.ANY)] * 2 + [pl.BlockSpec(memory_space=vmem)] * 2,
        out_specs=pl.BlockSpec(memory_space=vmem),
        scratch_shapes=[
            vmem((PLANE, depth, half), BF16),
            vmem((PLANE, depth, half), BF16),
            vmem((PLANE, depth, half), BF16),
            vmem((virtual, half), F32),
            vmem((4, coded, half), I16),
            vmem((4, coded, half), I16),
            vmem((4, coded, half), I16),
            vmem((4, coded, half), I16),
            vmem((2, NX, coded, half), I16),
            vmem((NX * slab, virtual), BF16),
            vmem((NX * slab, virtual), BF16),
            vmem((2, NX * slab, 128), BF16),
            vmem((2, NX * slab, 128), BF16),
            vmem((NY, 2, side, virtual // NY), F32),
            vmem((side, virtual // NY), F32),
            vmem((2, side, virtual // NY), F32),
            vmem((side, virtual // NY), F32),
            vmem((2, side, virtual // NY), F32),
            vmem((NZ, side, side), F32),
            vmem((4, side, side), F32),
            vmem((4, side, side), F32),
            dma((2,)),
            dma((PLANE,)),
            dma((PLANE,)),
            dma((PLANE,)),
            dma((PLANE,)),
            dma((PLANE,)),
            dma((PLANE,)),
            dma((8,)),
            dma((8,)),
            dma((4,)),
            dma((4,)),
            dma((4,)),
            dma((4,)),
            dma((4,)),
            dma((4,)),
            dma((8,)),
            dma((8,)),
        ],
        compiler_params=pltpu.CompilerParams(
            collective_id=1, has_side_effects=True, vmem_limit_bytes=48 * 1024 * 1024
        ),
        name="density",
    )(a_msg, b_msg, eb, ea)


def shards(three_index, occupied_energy, virtual_energy, pair_list):
    depth, orbitals, virtual = three_index.shape
    half = virtual // 2
    slab = virtual // NZ
    x, y, z, core = position()
    sibling_rows, listed = exchange(three_index, pair_list, half)
    pairs = listed[:, 0, 0:2]
    first, second = pairs[:, 0], pairs[:, 1]
    mine = lax.dynamic_slice_in_dim(three_index, core * half, half, axis=2)
    rows = jnp.stack([jnp.where(core == 0, mine, sibling_rows), jnp.where(core == 0, sibling_rows, mine)])
    split = rows.reshape(2, depth, PLANE, 2, half)
    odd = (first % 2 == 1)[None, None, :, None]
    left_rows = jnp.where(odd, split[:, :, :, 1], split[:, :, :, 0])
    a_msg = left_rows.transpose(2, 0, 1, 3).reshape(PLANE, 2 * depth, half)
    common = lax.dynamic_slice_in_dim(rows, pair_list[0, 1] // 2 * 2, 2, axis=2).reshape(2 * depth, 2, half)
    odd = (second % 2 == 1)[:, None, None]
    b_msg = jnp.where(odd, common[None, :, 1], common[None, :, 0])
    own_pair = lax.dynamic_index_in_dim(pairs, x * NY + y, 0, keepdims=False)
    shift_energy = occupied_energy[own_pair[0]] + occupied_energy[own_pair[1]]
    eb = lax.dynamic_slice_in_dim(virtual_energy, z * slab, slab)[:, None]
    ea = lax.dynamic_slice_in_dim(virtual_energy, core * half, half)[None, :] - shift_energy
    return density(a_msg, b_msg, eb, ea)


def solution(mesh):
    placed = (P(("occ", "aux"), None, None), P(), P(), P("occ", None))
    return jax.shard_map(shards, mesh=mesh, in_specs=placed, out_specs=P("aux", "occ"), check_vma=False)
```

```python
import functools

import jax
import jax.numpy as jnp
from jax import lax
from jax.experimental import pallas as pl
from jax.experimental.pallas import tpu as pltpu
from jax.sharding import PartitionSpec as P

MESH = pl.DeviceIdType.MESH
F32 = jnp.float32
BF16 = jnp.bfloat16
I16 = jnp.int16
I32 = jnp.int32
NX, NY, NZ = 4, 4, 8
PLANE = NX * NY
PAIRS = 16
ROWS = 16
LANES = 128
STEPS = NZ // 2


def position():
    occ, aux = lax.axis_index("occ"), lax.axis_index("aux")
    core = lax.rem(aux, 2)
    x = lax.rem(lax.div(aux, 2), NX)
    z = lax.div(aux, 2 * NX) * 4 + lax.rem(occ, 4)
    return x, lax.div(occ, 4), z, core


def device(x, y, z, core):
    return (y * 4 + lax.rem(z, 4), (lax.div(z, 4) * NX + x) * 2 + core)


def remote(src, dst, send, recv, dev):
    return pltpu.make_async_remote_copy(
        src_ref=src, dst_ref=dst, send_sem=send, recv_sem=recv, device_id=dev, device_id_type=MESH
    )


def loop(first, last, body):
    def step(k, carry):
        body(k)
        return carry

    lax.fori_loop(first, last, step, 0)


def dot_rows(a, b):
    return lax.dot_general(a, b, (((0,), (0,)), ((), ())), preferred_element_type=F32)


def coded_rows(rows, columns):
    return rows * (columns // LANES) + ROWS


def encode(block, ref):
    rows, columns = block.shape
    groups = columns // LANES
    top = jnp.maximum(jnp.max(jnp.abs(block), axis=0, keepdims=True), 1e-30)
    level = jnp.ceil(jnp.log(top) * 64.0)
    codes = jnp.round(block * (32000.0 * jnp.exp(level * (-1.0 / 64.0)))).astype(I32).astype(I16)
    row = lax.broadcasted_iota(I32, (ROWS, LANES), 0)
    tail = jnp.zeros((ROWS, LANES), F32)
    for g in range(groups):
        ref[g * rows : (g + 1) * rows, :] = codes[:, g * LANES : (g + 1) * LANES]
        tail = jnp.where(row == g, level[:, g * LANES : (g + 1) * LANES], tail)
    ref[groups * rows : groups * rows + ROWS, :] = tail.astype(I32).astype(I16)


def decode(ref, rows):
    groups = (ref.shape[0] - ROWS) // rows
    tail = ref[groups * rows : groups * rows + ROWS, :].astype(I32).astype(F32)
    scale = jnp.exp(tail * (1.0 / 64.0)) * (1.0 / 32000.0)
    parts = [
        ref[g * rows : (g + 1) * rows, :].astype(I32).astype(F32) * scale[g : g + 1, :] for g in range(groups)
    ]
    return jnp.concatenate(parts, axis=1)


def density_kernel(
    sizes, three, occupied, virtual, pairs, out,
    mine, table, pick, rows_in, a_msg, b_msg, a_in, b_in, b_sib, coulomb, up_out, up_in, down_out, down_in, amp,
    high, low, left_high, left_low, dens, y_up0, y_up1, y_down0, y_down1, part, z_up, z_down,
    own_sem, half_send, half_recv, t_send, t_recv, a_send, a_recv, b_send, b_recv, s_send, s_recv,
    ring_send, ring_recv, x_send, x_recv, c_send, c_recv, y_send, y_recv, z_send, z_recv,
):
    half, width, slab, side = sizes
    x, y, z, core = position()
    occ, aux = lax.axis_index("occ"), lax.axis_index("aux")
    me = x * NY + y
    sibling = device(x, y, z, 1 - core)
    above, below = device(x, y, lax.rem(z + 1, NZ), core), device(x, y, lax.rem(z + NZ - 1, NZ), core)
    block_rows = rows_in.shape[1]
    orbitals = block_rows // ROWS

    def occ_peer(k):
        return (lax.rem(occ + k, PAIRS), aux)

    def peer(k):
        to = lax.rem(me + k, PLANE)
        return device(lax.div(to, NY), lax.rem(to, NY), z, core)

    rest = block_rows // 2

    def places(which):
        return rows_in.at[2 * which], rows_in.at[1, pl.ds(pl.multiple_of(which * rest, rest), rest)]

    def columns_of(which):
        return pl.ds(pl.multiple_of(which * half, LANES), half)

    here = places(core)
    own = [
        pltpu.make_async_copy(three.at[:block_rows, columns_of(core)], here[0], own_sem.at[0]),
        pltpu.make_async_copy(three.at[block_rows:, columns_of(core)], here[1], own_sem.at[1]),
    ]
    for copy in own:
        copy.start()
    mine[...] = jnp.zeros_like(mine)
    mine[0:1, 0:2] = pairs[...]

    barrier = pltpu.get_barrier_semaphore()
    loop(1, PAIRS, lambda k: pl.semaphore_signal(barrier, inc=1, device_id=occ_peer(k), device_id_type=MESH))
    loop(1, PLANE, lambda k: pl.semaphore_signal(barrier, inc=1, device_id=peer(k), device_id_type=MESH))
    for other in (sibling, above, below):
        pl.semaphore_signal(barrier, inc=1, device_id=other, device_id_type=MESH)
    pl.semaphore_wait(barrier, PAIRS - 1 + PLANE - 1 + 3)

    def row_out(k):
        return remote(mine, table.at[occ], t_send.at[k], t_recv.at[k], occ_peer(k))

    def row_in(k):
        came = lax.rem(occ + PAIRS - k, PAIRS)
        return remote(mine, table.at[came], t_send.at[k], t_recv.at[k], occ_peer(k))

    loop(1, PAIRS, lambda k: row_out(k).start())
    given = [
        remote(three.at[:block_rows, columns_of(1 - core)], here[0], half_send.at[0], half_recv.at[0], sibling),
        remote(three.at[block_rows:, columns_of(1 - core)], here[1], half_send.at[1], half_recv.at[1], sibling),
    ]
    for copy in given:
        copy.start()
    table[occ] = mine[...]

    lane = lax.broadcasted_iota(I32, (slab, 2 * half), 1)
    row = lax.broadcasted_iota(I32, (slab, 2 * half), 0)
    eb = []
    for q in range(2):
        first = lax.div(z, 4) * half + q * width + lax.rem(z, 4) * slab
        eb.append(jnp.sum(jnp.where(lane == row + first, virtual[...], 0.0), axis=1, keepdims=True))
    ea = [
        virtual[:, pl.ds(pl.multiple_of(core * half + q * width, LANES), width)] for q in range(2)
    ]

    loop(1, PAIRS, lambda k: row_in(k).wait_recv())
    orbital = lax.broadcasted_iota(I32, (1, occupied.shape[1]), 1)
    shift = jnp.zeros((1, 1), F32)
    for n in range(2):
        chosen = jnp.where(orbital == table[me, 0:1, n : n + 1], occupied[...], 0.0)
        shift = shift + jnp.sum(chosen, axis=1, keepdims=True)
    lane = lax.broadcasted_iota(I32, (ROWS, block_rows), 1)
    row = lax.broadcasted_iota(I32, (ROWS, block_rows), 0) * orbitals
    for n in range(2):
        for p in range(PAIRS):
            hit = lane == row + table[p, 0:1, n : n + 1]
            pick[n, p * ROWS : (p + 1) * ROWS, :] = jnp.where(hit, 1.0, 0.0).astype(BF16)
    for copy in own:
        copy.wait()
    for copy in given:
        copy.wait_recv()

    def plane_out(msg, into, send, recv, q, k):
        return remote(
            msg.at[q, lax.rem(me + k, PLANE)], into.at[q, me], send.at[q, k], recv.at[q, k], peer(k)
        )

    def plane_in(msg, into, send, recv, q, k):
        came = lax.rem(me + PLANE - k, PLANE)
        return remote(msg.at[q, came], into.at[q, came], send.at[q, k], recv.at[q, k], peer(k))

    a_refs, b_refs = (a_msg, a_in, a_send, a_recv), (b_msg, b_in, b_send, b_recv)

    def pick_rows(n, msg):
        for g in range(3):
            value = jnp.dot(pick[n], rows_in[g], preferred_element_type=F32).astype(BF16)
            for q in range(2):
                msg[q, :, g * ROWS : (g + 1) * ROWS, :] = value[:, q * width : (q + 1) * width].reshape(
                    PAIRS, ROWS, width
                )

    def send_plane(refs, q):
        loop(1, PLANE, lambda k: plane_out(*refs, q, k).start())
        refs[1][q, me] = refs[0][q, me]

    def to_sibling(q, k):
        came = lax.rem(me + PLANE - k, PLANE)
        return remote(b_in.at[q, came], b_sib.at[q, came], s_send.at[q, k], s_recv.at[q, k], sibling)

    def take_b(q):
        to_sibling(q, 0).start()

        def pass_on(k):
            plane_in(*b_refs, q, k).wait_recv()
            to_sibling(q, k).start()

        loop(1, PLANE, pass_on)

    def take_a(q):
        loop(1, PLANE, lambda k: plane_in(*a_refs, q, k).wait_recv())

    def take_sibling(q):
        loop(0, PLANE, lambda k: to_sibling(q, k).wait_recv())

    pick_rows(1, b_msg)
    send_plane(b_refs, 0)
    pick_rows(0, a_msg)
    send_plane(a_refs, 0)
    send_plane(a_refs, 1)
    send_plane(b_refs, 1)

    chunks = [(0, 0), (0, 1), (1, 0), (1, 1)]

    def multiply(n):
        q, r = chunks[n]
        right = a_in[r].reshape(-1, width)
        for source, which in ((b_in, core), (b_sib, 1 - core)):
            part_rows = pl.ds(pl.multiple_of(which * width, width), width)
            coulomb[n, part_rows, :] = dot_rows(source[q].reshape(-1, width), right)

    def block(n, w):
        return coulomb[n, pl.ds(pl.multiple_of(w * slab, slab), slab), :]

    mid = slab // 2
    short = coded_rows(mid, width)
    ways = ((0, up_out, up_in, above), (1, down_out, down_in, below))

    def hop(n, way, t):
        _, box, into, to = ways[way]
        slot = (n, t, slice(0, short)) if t == 0 else (n, t)
        return remote(box.at[slot], into.at[slot], ring_send.at[n, way, t], ring_recv.at[n, way, t], to)

    def ring(n, t):
        for way, box, into, _ in ways:
            w = lax.rem(z + 4 + t, NZ) if way else lax.rem(z + 4 - t, NZ)
            value = block(n, w)
            if t == 0:
                encode(value[mid:] if way else value[:mid], box.at[n, 0, :short])
            else:
                hop(n, way, t - 1).wait_recv()
                if t == 1:
                    came = decode(into.at[n, 0, :short], mid)
                    halves = [value[:mid], value[mid:]]
                    halves[way] = halves[way] + came
                    value = jnp.concatenate(halves, axis=0)
                else:
                    value = value + decode(into.at[n, t - 1], slab)
                encode(value, box.at[n, t])
            hop(n, way, t).start()

    x_next, x_prev, x_far = lax.rem(x + 1, NX), lax.rem(x + NX - 1, NX), lax.rem(x + 2, NX)
    lines = (x_next, x_prev, x_far)

    def line_out(n, i):
        q, r = chunks[n]
        ref = amp.at[core, r, x, q]
        return remote(ref, ref, x_send.at[n, i], x_recv.at[n, i], device(lines[i], y, z, core))

    def line_in(n, i):
        q, r = chunks[n]
        ref = amp.at[core, r, (x_prev, x_next, x_far)[i], q]
        return remote(ref, ref, x_send.at[n, i], x_recv.at[n, i], device(lines[i], y, z, core))

    def cross(n, i, which):
        q, r = chunks[n]
        ref = amp.at[which, r, (x_prev, x_next, x_far, x)[i], q]
        return remote(ref, ref, c_send.at[n, i], c_recv.at[n, i], sibling)

    def amplitude(n):
        q, r = chunks[n]
        hop(n, 0, STEPS - 1).wait_recv()
        hop(n, 1, STEPS - 1).wait_recv()
        total = block(n, z) + decode(up_in.at[n, STEPS - 1], slab) + decode(down_in.at[n, STEPS - 1], slab)
        encode(-total / (eb[q] + ea[r] - shift), amp.at[core, r, x, q])
        for i in range(3):
            line_out(n, i).start()
        cross(n, 3, core).start()

    def forward(n):
        for i in range(3):
            line_in(n, i).wait_recv()
            cross(n, i, core).start()

    turn = x * 2 + core
    turn_chunk, turn_shift = lax.div(turn, 4), lax.rem(width - side * lax.rem(turn, 4), width)

    def unpack(n):
        q, r = chunks[n]
        for i in range(4):
            cross(n, i, 1 - core).wait_recv()
        for h in range(2):
            for k in range(NX):
                value = decode(amp.at[h, r, k, q], slab)
                rows = slice((k * 2 + q) * slab, (k * 2 + q + 1) * slab)
                columns = slice(h * half + r * width, h * half + (r + 1) * width)
                top = value.astype(BF16)
                high[rows, columns] = top
                low[rows, columns] = (value - top.astype(F32)).astype(BF16)

    take_b(0)
    take_a(0)
    take_sibling(0)
    multiply(0)
    ring(0, 0)
    ring(0, 1)
    ring(0, 2)
    take_a(1)
    multiply(1)
    ring(1, 0)
    ring(0, 3)
    ring(1, 1)
    amplitude(0)
    take_b(1)
    take_sibling(1)
    multiply(2)
    ring(2, 0)
    ring(1, 2)
    multiply(3)
    ring(3, 0)
    ring(2, 1)
    ring(1, 3)
    ring(3, 1)
    forward(0)
    amplitude(1)
    ring(2, 2)
    ring(3, 2)
    ring(2, 3)
    unpack(0)
    forward(1)
    ring(3, 3)
    amplitude(2)
    unpack(1)
    amplitude(3)
    forward(2)
    unpack(2)
    forward(3)
    unpack(3)

    for h in range(2):
        for k in range(NX):
            for q in range(2):
                rows = slice((k * 2 + q) * slab, (k * 2 + q + 1) * slab)
                turned = pltpu.roll(decode(amp.at[h, turn_chunk, k, q], slab), turn_shift, 1)[:, 0:LANES]
                top = turned.astype(BF16)
                left_high[h, rows, :] = top
                left_low[h, rows, :] = (turned - top.astype(F32)).astype(BF16)
    wide = dens.shape[3]
    for h in range(2):
        for n in range(NY):
            columns = slice(n * wide, (n + 1) * wide)
            total = dot_rows(left_high[h], low[:, columns]) + dot_rows(left_low[h], high[:, columns])
            total = total + dot_rows(left_low[h], low[:, columns])
            dens[n, h] = (total + dot_rows(left_high[h], high[:, columns]))[0:side, :]

    y_next, y_prev, y_far = lax.rem(y + 1, NY), lax.rem(y + NY - 1, NY), lax.rem(y + 2, NY)
    north, south = device(x, y_next, z, core), device(x, y_prev, z, core)
    first = remote(dens.at[y_far, 0], y_up0, y_send.at[0], y_recv.at[0], north)
    second = remote(dens.at[y_far, 1], y_down0, y_send.at[1], y_recv.at[1], south)
    first.start()
    second.start()
    first.wait_recv()
    dens[y_next, 0] = dens[y_next, 0] + y_up0[...]
    third = remote(dens.at[y_next], y_up1, y_send.at[2], y_recv.at[2], north)
    third.start()
    second.wait_recv()
    dens[y_prev, 1] = dens[y_prev, 1] + y_down0[...]
    fourth = remote(dens.at[y_prev], y_down1, y_send.at[3], y_recv.at[3], south)
    fourth.start()
    third.wait_recv()
    fourth.wait_recv()
    for h in range(2):
        total = dens[y, h] + y_up1[h] + y_down1[h]
        for n in range(4):
            part[h * 4 + n] = total[:, n * side : (n + 1) * side]

    far_z = lax.rem(z + 4, NZ)
    cut = side // 2
    up_z = [remote(part.at[far_z, :cut], z_up.at[0, :cut], z_send.at[0], z_recv.at[0], above)]
    down_z = [remote(part.at[far_z, cut:], z_down.at[0, cut:], z_send.at[4], z_recv.at[4], below)]
    up_z[0].start()
    down_z[0].start()
    for t in range(1, STEPS):
        for way, sent, into, w, to in (
            (0, up_z, z_up, lax.rem(z + 4 - t, NZ), above),
            (1, down_z, z_down, lax.rem(z + 4 + t, NZ), below),
        ):
            sent[t - 1].wait_recv()
            if t > 1:
                part[w] = part[w] + into[t - 1]
            elif way:
                part[w, cut:] = part[w, cut:] + into[0, cut:]
            else:
                part[w, :cut] = part[w, :cut] + into[0, :cut]
            sent.append(remote(part.at[w], into.at[t], z_send.at[4 * way + t], z_recv.at[4 * way + t], to))
            sent[t].start()
    up_z[3].wait_recv()
    down_z[3].wait_recv()
    out[...] = part[z] + z_up[3] + z_down[3]

    for copy in given + [first, second, third, fourth] + up_z + down_z:
        copy.wait_send()
    loop(1, PAIRS, lambda k: row_out(k).wait_send())
    for q in range(2):
        loop(1, PLANE, lambda k, q=q: plane_out(*b_refs, q, k).wait_send())
        loop(1, PLANE, lambda k, q=q: plane_out(*a_refs, q, k).wait_send())
        loop(0, PLANE, lambda k, q=q: to_sibling(q, k).wait_send())
    for n in range(4):
        for way in range(2):
            for t in range(STEPS):
                hop(n, way, t).wait_send()
        for i in range(3):
            line_out(n, i).wait_send()
        for i in range(4):
            cross(n, i, core).wait_send()


def shards(three_index, occupied_energy, virtual_energy, pair_list):
    depth, orbitals, virtual = three_index.shape
    half = virtual // 2
    width = half // 2
    slab = width * 2 // NZ
    side = virtual // 16
    block_rows = ROWS * orbitals
    coded = coded_rows(slab, width)
    dma, vmem = pltpu.SemaphoreType.DMA, pltpu.VMEM
    inside = pl.BlockSpec(memory_space=vmem)
    message = (2, PLANE, 2 * depth, width)
    ring_box = (4, STEPS, coded, LANES)
    scratch = [
        vmem((8, LANES), I32),
        vmem((PAIRS, 8, LANES), I32),
        vmem((2, PAIRS * ROWS, block_rows), BF16),
        vmem((3, block_rows, half), BF16),
        *[vmem(message, BF16)] * 5,
        vmem((4, 2 * width, width), F32),
        *[vmem(ring_box, I16)] * 4,
        vmem((2, 2, NX, 2, coded, LANES), I16),
        *[vmem((NX * 2 * slab, virtual), BF16)] * 2,
        *[vmem((2, NX * 2 * slab, LANES), BF16)] * 2,
        vmem((NY, 2, side, virtual // NY), F32),
        *[vmem((side, virtual // NY), F32), vmem((2, side, virtual // NY), F32)] * 2,
        vmem((NZ, side, side), F32),
        *[vmem((STEPS, side, side), F32)] * 2,
        dma((2,)),
        *[dma((2,))] * 2,
        *[dma((PAIRS,))] * 2,
        *[dma((2, PLANE))] * 6,
        *[dma((4, 2, STEPS))] * 2,
        *[dma((4, 3))] * 2,
        *[dma((4, 4))] * 2,
        *[dma((4,))] * 2,
        *[dma((8,))] * 2,
    ]
    return pl.pallas_call(
        functools.partial(density_kernel, (half, width, slab, side)),
        out_shape=jax.ShapeDtypeStruct((side, side), F32),
        in_specs=[pl.BlockSpec(memory_space=pl.ANY), inside, inside, inside],
        out_specs=inside,
        scratch_shapes=scratch,
        compiler_params=pltpu.CompilerParams(
            collective_id=0, has_side_effects=True, vmem_limit_bytes=48 * 1024 * 1024
        ),
        name="density",
    )(
        three_index.reshape(depth * orbitals, virtual),
        occupied_energy.reshape(1, -1),
        virtual_energy.reshape(1, -1),
        pair_list,
    )


def solution(mesh):
    placed = (P(("occ", "aux"), None, None), P(), P(), P("occ", None))
    return jax.shard_map(shards, mesh=mesh, in_specs=placed, out_specs=P("aux", "occ"), check_vma=False)
```

```python
import functools

import jax
import jax.numpy as jnp
from jax import lax
from jax.experimental import pallas as pl
from jax.experimental.pallas import tpu as pltpu
from jax.sharding import PartitionSpec as P

MESH = pl.DeviceIdType.MESH
F32 = jnp.float32
BF16 = jnp.bfloat16
I16 = jnp.int16
I32 = jnp.int32
NX, NY, NZ = 4, 4, 8
PLANE = NX * NY
PAIRS = 16
ROWS = 16
LANES = 128
STEPS = NZ // 2


def position():
    occ, aux = lax.axis_index("occ"), lax.axis_index("aux")
    core = lax.rem(aux, 2)
    x = lax.rem(lax.div(aux, 2), NX)
    z = lax.div(aux, 2 * NX) * 4 + lax.rem(occ, 4)
    return x, lax.div(occ, 4), z, core


def device(x, y, z, core):
    return (y * 4 + lax.rem(z, 4), (lax.div(z, 4) * NX + x) * 2 + core)


def remote(src, dst, send, recv, dev):
    return pltpu.make_async_remote_copy(
        src_ref=src, dst_ref=dst, send_sem=send, recv_sem=recv, device_id=dev, device_id_type=MESH
    )


def loop(first, last, body):
    def step(k, carry):
        body(k)
        return carry

    lax.fori_loop(first, last, step, 0)


def dot_rows(a, b):
    return lax.dot_general(a, b, (((0,), (0,)), ((), ())), preferred_element_type=F32)


def coded_rows(rows, columns):
    return rows * (columns // LANES) + ROWS


def encode(block, ref):
    rows, columns = block.shape
    groups = columns // LANES
    top = jnp.maximum(jnp.max(jnp.abs(block), axis=0, keepdims=True), 1e-30)
    level = jnp.ceil(jnp.log(top) * 64.0)
    codes = jnp.round(block * (32000.0 * jnp.exp(level * (-1.0 / 64.0)))).astype(I32).astype(I16)
    row = lax.broadcasted_iota(I32, (ROWS, LANES), 0)
    tail = jnp.zeros((ROWS, LANES), F32)
    for g in range(groups):
        ref[g * rows : (g + 1) * rows, :] = codes[:, g * LANES : (g + 1) * LANES]
        tail = jnp.where(row == g, level[:, g * LANES : (g + 1) * LANES], tail)
    ref[groups * rows : groups * rows + ROWS, :] = tail.astype(I32).astype(I16)


def decode(ref, rows):
    groups = (ref.shape[0] - ROWS) // rows
    tail = ref[groups * rows : groups * rows + ROWS, :].astype(I32).astype(F32)
    scale = jnp.exp(tail * (1.0 / 64.0)) * (1.0 / 32000.0)
    parts = [
        ref[g * rows : (g + 1) * rows, :].astype(I32).astype(F32) * scale[g : g + 1, :] for g in range(groups)
    ]
    return jnp.concatenate(parts, axis=1)


def density_kernel(
    sizes, three, occupied_in, virtual_in, pairs_in, out,
    occupied, virtual, pairs, mine, table, pick, rows_in, a_msg, b_msg, a_in, b_in, b_sib, coulomb, up_out, up_in, down_out, down_in, amp,
    high, low, left_high, left_low, dens_a, y_up, y_down, part, z_up, z_down, dens_b, w_up, w_down, v_in,
    own_sem, half_send, half_recv, t_send, t_recv, a_send, a_recv, b_send, b_recv, s_send, s_recv,
    ring_send, ring_recv, x_send, x_recv, c_send, c_recv, y_send, y_recv, z_send, z_recv, w_send, w_recv, v_send, v_recv,
):
    half, width, slab, side = sizes
    x, y, z, core = position()
    occ, aux = lax.axis_index("occ"), lax.axis_index("aux")
    me = x * NY + y
    sibling = device(x, y, z, 1 - core)
    above, below = device(x, y, lax.rem(z + 1, NZ), core), device(x, y, lax.rem(z + NZ - 1, NZ), core)
    block_rows = rows_in.shape[1]
    orbitals = block_rows // ROWS

    def occ_peer(k):
        return (lax.rem(occ + k, PAIRS), aux)

    def peer(k):
        to = lax.rem(me + k, PLANE)
        return device(lax.div(to, NY), lax.rem(to, NY), z, core)

    rest = block_rows // 2

    def places(which):
        return rows_in.at[2 * which], rows_in.at[1, pl.ds(pl.multiple_of(which * rest, rest), rest)]

    def columns_of(which):
        return pl.ds(pl.multiple_of(which * half, LANES), half)

    here = places(core)
    own = [
        pltpu.make_async_copy(three.at[:block_rows, columns_of(core)], here[0], own_sem.at[0]),
        pltpu.make_async_copy(three.at[block_rows:, columns_of(core)], here[1], own_sem.at[1]),
    ]
    small = [
        pltpu.make_async_copy(pairs_in, pairs, own_sem.at[2]),
        pltpu.make_async_copy(virtual_in, virtual.at[0], own_sem.at[3]),
        pltpu.make_async_copy(occupied_in, occupied.at[0], own_sem.at[4]),
    ]
    for copy in small + own:
        copy.start()
    mine[...] = jnp.zeros_like(mine)

    barrier = pltpu.get_barrier_semaphore()
    loop(1, PAIRS, lambda k: pl.semaphore_signal(barrier, inc=1, device_id=occ_peer(k), device_id_type=MESH))
    loop(1, PLANE, lambda k: pl.semaphore_signal(barrier, inc=1, device_id=peer(k), device_id_type=MESH))
    for other in (sibling, above, below):
        pl.semaphore_signal(barrier, inc=1, device_id=other, device_id_type=MESH)
    small[0].wait()
    mine[0:1, 0:2] = pairs[...]
    pl.semaphore_wait(barrier, PAIRS - 1 + PLANE - 1 + 3)

    def row_out(k):
        return remote(mine, table.at[occ], t_send.at[k], t_recv.at[k], occ_peer(k))

    def row_in(k):
        came = lax.rem(occ + PAIRS - k, PAIRS)
        return remote(mine, table.at[came], t_send.at[k], t_recv.at[k], occ_peer(k))

    loop(1, PAIRS, lambda k: row_out(k).start())
    given = [
        remote(three.at[:block_rows, columns_of(1 - core)], here[0], half_send.at[0], half_recv.at[0], sibling),
        remote(three.at[block_rows:, columns_of(1 - core)], here[1], half_send.at[1], half_recv.at[1], sibling),
    ]
    for copy in given:
        copy.start()
    table[occ] = mine[...]

    small[1].wait()
    small[2].wait()
    lane = lax.broadcasted_iota(I32, (slab, 2 * half), 1)
    row = lax.broadcasted_iota(I32, (slab, 2 * half), 0)
    eb = []
    for q in range(2):
        first = lax.div(z, 4) * half + q * width + lax.rem(z, 4) * slab
        eb.append(jnp.sum(jnp.where(lane == row + first, virtual[...], 0.0), axis=1, keepdims=True))
    ea = [
        virtual[:, pl.ds(pl.multiple_of(core * half + q * width, LANES), width)] for q in range(2)
    ]

    loop(1, PAIRS, lambda k: row_in(k).wait_recv())
    orbital = lax.broadcasted_iota(I32, (1, occupied.shape[1]), 1)
    shift = jnp.zeros((1, 1), F32)
    for n in range(2):
        chosen = jnp.where(orbital == table[me, 0:1, n : n + 1], occupied[...], 0.0)
        shift = shift + jnp.sum(chosen, axis=1, keepdims=True)
    lane = lax.broadcasted_iota(I32, (ROWS, block_rows), 1)
    row = lax.broadcasted_iota(I32, (ROWS, block_rows), 0) * orbitals
    for n in range(2):
        for p in range(PAIRS):
            hit = lane == row + table[p, 0:1, n : n + 1]
            pick[n, p * ROWS : (p + 1) * ROWS, :] = jnp.where(hit, 1.0, 0.0).astype(BF16)
    for copy in own:
        copy.wait()
    for copy in given:
        copy.wait_recv()

    def plane_out(msg, into, send, recv, q, k):
        return remote(
            msg.at[q, lax.rem(me + k, PLANE)], into.at[q, me], send.at[q, k], recv.at[q, k], peer(k)
        )

    def plane_in(msg, into, send, recv, q, k):
        came = lax.rem(me + PLANE - k, PLANE)
        return remote(msg.at[q, came], into.at[q, came], send.at[q, k], recv.at[q, k], peer(k))

    a_refs, b_refs = (a_msg, a_in, a_send, a_recv), (b_msg, b_in, b_send, b_recv)

    def pick_rows(n, msg):
        for g in range(3):
            value = jnp.dot(pick[n], rows_in[g], preferred_element_type=F32).astype(BF16)
            for q in range(2):
                msg[q, :, g * ROWS : (g + 1) * ROWS, :] = value[:, q * width : (q + 1) * width].reshape(
                    PAIRS, ROWS, width
                )

    def send_plane(refs):
        loop(1, PLANE, lambda k: plane_out(*refs, 0, k).start())
        for q in range(2):
            refs[1][q, me] = refs[0][q, me]

    def to_sibling(q, k):
        came = lax.rem(me + PLANE - k, PLANE)
        return remote(b_in.at[q, came], b_sib.at[q, came], s_send.at[q, k], s_recv.at[q, k], sibling)

    def take_b(q):
        to_sibling(q, 0).start()

        def pass_on(k):
            plane_in(*b_refs, q, k).wait_recv()
            to_sibling(q, k).start()
            if q == 0:
                plane_out(*b_refs, 0, k).wait_send()
                plane_out(*a_refs, 1, k).start()

        loop(1, PLANE, pass_on)

    def take_a(q):
        def take(k):
            plane_in(*a_refs, q, k).wait_recv()
            if q == 0:
                plane_out(*a_refs, 0, k).wait_send()
                plane_out(*b_refs, 1, k).start()

        loop(1, PLANE, take)

    def take_sibling(q):
        loop(0, PLANE, lambda k: to_sibling(q, k).wait_recv())

    pick_rows(1, b_msg)
    send_plane(b_refs)
    pick_rows(0, a_msg)
    send_plane(a_refs)

    chunks = [(0, 0), (0, 1), (1, 0), (1, 1)]

    def multiply(n):
        q, r = chunks[n]
        right = a_in[r].reshape(-1, width)
        for source, which in ((b_in, core), (b_sib, 1 - core)):
            part_rows = pl.ds(pl.multiple_of(which * width, width), width)
            coulomb[n, part_rows, :] = dot_rows(source[q].reshape(-1, width), right)

    def block(n, w):
        return coulomb[n, pl.ds(pl.multiple_of(w * slab, slab), slab), :]

    mid = slab // 2
    short = coded_rows(mid, width)
    ways = ((0, up_out, up_in, above), (1, down_out, down_in, below))

    def hop(n, way, t):
        _, box, into, to = ways[way]
        slot = (n, t, slice(0, short)) if t == 0 else (n, t)
        return remote(box.at[slot], into.at[slot], ring_send.at[n, way, t], ring_recv.at[n, way, t], to)

    def ring(n, t):
        for way, box, into, _ in ways:
            w = lax.rem(z + 4 + t, NZ) if way else lax.rem(z + 4 - t, NZ)
            value = block(n, w)
            if t == 0:
                encode(value[mid:] if way else value[:mid], box.at[n, 0, :short])
            else:
                hop(n, way, t - 1).wait_recv()
                if t == 1:
                    came = decode(into.at[n, 0, :short], mid)
                    halves = [value[:mid], value[mid:]]
                    halves[way] = halves[way] + came
                    value = jnp.concatenate(halves, axis=0)
                else:
                    value = value + decode(into.at[n, t - 1], slab)
                encode(value, box.at[n, t])
            hop(n, way, t).start()

    x_next, x_prev, x_far = lax.rem(x + 1, NX), lax.rem(x + NX - 1, NX), lax.rem(x + 2, NX)
    lines = (x_next, x_prev, x_far)

    def line_out(n, i):
        q, r = chunks[n]
        ref = amp.at[core, r, x, q]
        return remote(ref, ref, x_send.at[n, i], x_recv.at[n, i], device(lines[i], y, z, core))

    def line_in(n, i):
        q, r = chunks[n]
        ref = amp.at[core, r, (x_prev, x_next, x_far)[i], q]
        return remote(ref, ref, x_send.at[n, i], x_recv.at[n, i], device(lines[i], y, z, core))

    def cross(n, i, which):
        q, r = chunks[n]
        ref = amp.at[which, r, (x_prev, x_next, x_far, x)[i], q]
        return remote(ref, ref, c_send.at[n, i], c_recv.at[n, i], sibling)

    def amplitude(n):
        q, r = chunks[n]
        hop(n, 0, STEPS - 1).wait_recv()
        hop(n, 1, STEPS - 1).wait_recv()
        total = block(n, z) + decode(up_in.at[n, STEPS - 1], slab) + decode(down_in.at[n, STEPS - 1], slab)
        encode(-total / (eb[q] + ea[r] - shift), amp.at[core, r, x, q])
        for i in range(3):
            line_out(n, i).start()
        cross(n, 3, core).start()

    def forward(n):
        for i in range(3):
            line_in(n, i).wait_recv()
            cross(n, i, core).start()

    turn = x * 2 + core
    turn_chunk, turn_shift = lax.div(turn, 4), lax.rem(width - side * lax.rem(turn, 4), width)

    def unpack(n):
        q, r = chunks[n]
        for i in range(4):
            cross(n, i, 1 - core).wait_recv()
        for h in range(2):
            for k in range(NX):
                value = decode(amp.at[h, r, k, q], slab)
                rows = slice((k * 2 + q) * slab, (k * 2 + q + 1) * slab)
                columns = slice(h * half + r * width, h * half + (r + 1) * width)
                top = value.astype(BF16)
                high[rows, columns] = top
                low[rows, columns] = (value - top.astype(F32)).astype(BF16)

    take_b(0)
    take_a(0)
    take_sibling(0)
    multiply(0)
    ring(0, 0)
    ring(0, 1)
    take_a(1)
    multiply(1)
    ring(1, 0)
    ring(0, 2)
    ring(1, 1)
    ring(0, 3)
    take_b(1)
    ring(1, 2)
    take_sibling(1)
    multiply(2)
    ring(2, 0)
    amplitude(0)
    multiply(3)
    ring(3, 0)
    ring(1, 3)
    ring(2, 1)
    ring(3, 1)
    forward(0)
    amplitude(1)
    ring(2, 2)
    ring(3, 2)
    unpack(0)
    ring(2, 3)
    forward(1)
    ring(3, 3)
    amplitude(2)
    amplitude(3)
    unpack(1)
    forward(2)
    unpack(2)
    forward(3)
    unpack(3)

    for h in range(2):
        for k in range(NX):
            for q in range(2):
                rows = slice((k * 2 + q) * slab, (k * 2 + q + 1) * slab)
                turned = pltpu.roll(decode(amp.at[h, turn_chunk, k, q], slab), turn_shift, 1)[:, 0:LANES]
                top = turned.astype(BF16)
                left_high[h, rows, :] = top
                left_low[h, rows, :] = (turned - top.astype(F32)).astype(BF16)
    wide = dens_a.shape[3]
    cut = side // 2
    for h in range(2):
        for n in range(NY):
            columns = slice(n * wide, (n + 1) * wide)
            total = dot_rows(left_high[h], low[:, columns]) + dot_rows(left_low[h], high[:, columns])
            total = total + dot_rows(left_low[h], low[:, columns])
            total = total + dot_rows(left_high[h], high[:, columns])
            dens_a[n, h] = total[0:cut, :]
            for i in range(4):
                dens_b[h * 4 + i, n] = total[cut:side, i * side : (i + 1) * side]

    y_next, y_prev, y_far = lax.rem(y + 1, NY), lax.rem(y + NY - 1, NY), lax.rem(y + 2, NY)
    north, south = device(x, y_next, z, core), device(x, y_prev, z, core)
    up_y = [
        remote(dens_a.at[w, h], y_up.at[i], y_send.at[i], y_recv.at[i], north)
        for i, (w, h) in enumerate(((y_far, 0), (y_next, 1), (y_next, 0)))
    ]
    down_y = [
        remote(dens_a.at[w, h], y_down.at[i], y_send.at[3 + i], y_recv.at[3 + i], south)
        for i, (w, h) in enumerate(((y_far, 1), (y_prev, 0), (y_prev, 1)))
    ]

    def z_hop(rows, boxes, sems, way, t):
        into, to = boxes[way], (above, below)[way]
        w = lax.rem(z + 4 + t, NZ) if way else lax.rem(z + 4 - t, NZ)
        part_of = rows.shape[1] // 2
        some = (pl.ds(part_of, part_of) if way else pl.ds(0, part_of)) if t == 0 else slice(None)
        return remote(
            rows.at[w, some], into.at[t, some], sems[0].at[4 * way + t], sems[1].at[4 * way + t], to
        )

    def z_step(rows, boxes, sems, t):
        part_of = rows.shape[1] // 2
        for way in range(2):
            w = lax.rem(z + 4 + t, NZ) if way else lax.rem(z + 4 - t, NZ)
            if t > 0:
                z_hop(rows, boxes, sems, way, t - 1).wait_recv()
                some = (slice(part_of, None) if way else slice(0, part_of)) if t == 1 else slice(None)
                rows[w, some] = rows[w, some] + boxes[way][t - 1, some]
            z_hop(rows, boxes, sems, way, t).start()

    def z_last(rows, boxes, sems):
        z_hop(rows, boxes, sems, 0, STEPS - 1).wait_recv()
        z_hop(rows, boxes, sems, 1, STEPS - 1).wait_recv()
        return rows[z] + boxes[0][STEPS - 1] + boxes[1][STEPS - 1]

    over_a = (part, (z_up, z_down), (z_send, z_recv))
    over_b = (dens_b, (w_up, w_down), (w_send, w_recv))
    for copy in (up_y[0], down_y[0], up_y[1], down_y[1]):
        copy.start()
    z_step(*over_b, 0)
    up_y[0].wait_recv()
    dens_a[y_next, 0] = dens_a[y_next, 0] + y_up[0]
    up_y[2].start()
    down_y[0].wait_recv()
    dens_a[y_prev, 1] = dens_a[y_prev, 1] + y_down[0]
    down_y[2].start()
    z_step(*over_b, 1)
    z_step(*over_b, 2)
    for copy in up_y[1:] + down_y[1:]:
        copy.wait_recv()
    for h, came in ((0, y_up[2] + y_down[1]), (1, y_up[1] + y_down[2])):
        total = dens_a[y, h] + came
        for i in range(4):
            part[h * 4 + i] = total[:, i * side : (i + 1) * side]
    z_step(*over_a, 0)
    z_step(*over_b, 3)
    z_step(*over_a, 1)
    summed = z_last(*over_b)
    for n in range(NY):
        v_in[0, n] = summed[n]

    def column(i):
        w = (y_next, y_prev, y_far)[i]
        return remote(v_in.at[0, w], v_in.at[1 + i, 0], v_send.at[i], v_recv.at[i], device(x, w, z, core))

    for i in range(3):
        column(i).start()
    z_step(*over_a, 2)
    z_step(*over_a, 3)
    for i in range(3):
        column(i).wait_recv()
    out[cut:, :] = v_in[0, y] + v_in[1, 0] + v_in[2, 0] + v_in[3, 0]
    out[:cut, :] = z_last(*over_a)

    for copy in given + up_y + down_y:
        copy.wait_send()
    for over in (over_a, over_b):
        for way in range(2):
            for t in range(STEPS):
                z_hop(*over, way, t).wait_send()
    for i in range(3):
        column(i).wait_send()
    loop(1, PAIRS, lambda k: row_out(k).wait_send())
    loop(1, PLANE, lambda k: plane_out(*b_refs, 1, k).wait_send())
    loop(1, PLANE, lambda k: plane_out(*a_refs, 1, k).wait_send())
    for q in range(2):
        loop(0, PLANE, lambda k, q=q: to_sibling(q, k).wait_send())
    for n in range(4):
        for way in range(2):
            for t in range(STEPS):
                hop(n, way, t).wait_send()
        for i in range(3):
            line_out(n, i).wait_send()
        for i in range(4):
            cross(n, i, core).wait_send()


def shards(three_index, occupied_energy, virtual_energy, pair_list):
    depth, orbitals, virtual = three_index.shape
    half = virtual // 2
    width = half // 2
    slab = width * 2 // NZ
    side = virtual // 16
    block_rows = ROWS * orbitals
    coded = coded_rows(slab, width)
    dma, vmem = pltpu.SemaphoreType.DMA, pltpu.VMEM
    inside = pl.BlockSpec(memory_space=vmem)
    message = (2, PLANE, 2 * depth, width)
    ring_box = (4, STEPS, coded, LANES)
    cut = side // 2
    scratch = [
        vmem((1, orbitals), F32),
        vmem((1, virtual), F32),
        vmem((1, 2), I32),
        vmem((8, LANES), I32),
        vmem((PAIRS, 8, LANES), I32),
        vmem((2, PAIRS * ROWS, block_rows), BF16),
        vmem((3, block_rows, half), BF16),
        *[vmem(message, BF16)] * 5,
        vmem((4, 2 * width, width), F32),
        *[vmem(ring_box, I16)] * 4,
        vmem((2, 2, NX, 2, coded, LANES), I16),
        *[vmem((NX * 2 * slab, virtual), BF16)] * 2,
        *[vmem((2, NX * 2 * slab, LANES), BF16)] * 2,
        vmem((NY, 2, cut, virtual // NY), F32),
        *[vmem((3, cut, virtual // NY), F32)] * 2,
        vmem((NZ, cut, side), F32),
        *[vmem((STEPS, cut, side), F32)] * 2,
        vmem((NZ, NY, cut, side), F32),
        *[vmem((STEPS, NY, cut, side), F32)] * 2,
        vmem((4, NY, cut, side), F32),
        dma((5,)),
        *[dma((2,))] * 2,
        *[dma((PAIRS,))] * 2,
        *[dma((2, PLANE))] * 6,
        *[dma((4, 2, STEPS))] * 2,
        *[dma((4, 3))] * 2,
        *[dma((4, 4))] * 2,
        *[dma((6,))] * 2,
        *[dma((8,))] * 4,
        *[dma((3,))] * 2,
    ]
    return pl.pallas_call(
        functools.partial(density_kernel, (half, width, slab, side)),
        out_shape=jax.ShapeDtypeStruct((side, side), F32),
        in_specs=[pl.BlockSpec(memory_space=pltpu.HBM)] * 4,
        out_specs=inside,
        scratch_shapes=scratch,
        compiler_params=pltpu.CompilerParams(
            collective_id=0, has_side_effects=True, vmem_limit_bytes=62 * 1024 * 1024
        ),
        name="density",
    )(
        three_index.reshape(depth * orbitals, virtual),
        occupied_energy,
        virtual_energy,
        pair_list,
    )


def solution(mesh):
    placed = (P(("occ", "aux"), None, None), P(), P(), P("occ", None))
    return jax.shard_map(shards, mesh=mesh, in_specs=placed, out_specs=P("aux", "occ"), check_vma=False)
```

```python
import functools

import jax
import jax.numpy as jnp
from jax import lax
from jax.experimental import pallas as pl
from jax.experimental.pallas import tpu as pltpu
from jax.sharding import PartitionSpec as P

MESH = pl.DeviceIdType.MESH
F32 = jnp.float32
BF16 = jnp.bfloat16
I16 = jnp.int16
I32 = jnp.int32
NX, NY, NZ = 4, 4, 8
PLANE = NX * NY
PAIRS = 16
ROWS = 16
LANES = 128
STEPS = NZ // 2


def position():
    occ, aux = lax.axis_index("occ"), lax.axis_index("aux")
    core = lax.rem(aux, 2)
    x = lax.rem(lax.div(aux, 2), NX)
    z = lax.div(aux, 2 * NX) * 4 + lax.rem(occ, 4)
    return x, lax.div(occ, 4), z, core


def device(x, y, z, core):
    return (y * 4 + lax.rem(z, 4), (lax.div(z, 4) * NX + x) * 2 + core)


def remote(src, dst, send, recv, dev):
    return pltpu.make_async_remote_copy(
        src_ref=src, dst_ref=dst, send_sem=send, recv_sem=recv, device_id=dev, device_id_type=MESH
    )


def loop(first, last, body):
    def step(k, carry):
        body(k)
        return carry

    lax.fori_loop(first, last, step, 0)


def upper_rows(side):
    return side * 7 // 12 // 8 * 8


def dot_rows(a, b):
    return lax.dot_general(a, b, (((0,), (0,)), ((), ())), preferred_element_type=F32)


def coded_rows(rows, columns):
    return rows * (columns // LANES) + ROWS


def encode(block, ref):
    rows, columns = block.shape
    groups = columns // LANES
    top = jnp.maximum(jnp.max(jnp.abs(block), axis=0, keepdims=True), 1e-30)
    level = jnp.ceil(jnp.log(top) * 64.0)
    codes = jnp.round(block * (32000.0 * jnp.exp(level * (-1.0 / 64.0)))).astype(I32).astype(I16)
    row = lax.broadcasted_iota(I32, (ROWS, LANES), 0)
    tail = jnp.zeros((ROWS, LANES), F32)
    for g in range(groups):
        ref[g * rows : (g + 1) * rows, :] = codes[:, g * LANES : (g + 1) * LANES]
        tail = jnp.where(row == g, level[:, g * LANES : (g + 1) * LANES], tail)
    ref[groups * rows : groups * rows + ROWS, :] = tail.astype(I32).astype(I16)


def decode(ref, rows):
    groups = (ref.shape[0] - ROWS) // rows
    tail = ref[groups * rows : groups * rows + ROWS, :].astype(I32).astype(F32)
    scale = jnp.exp(tail * (1.0 / 64.0)) * (1.0 / 32000.0)
    parts = [
        ref[g * rows : (g + 1) * rows, :].astype(I32).astype(F32) * scale[g : g + 1, :] for g in range(groups)
    ]
    return jnp.concatenate(parts, axis=1)


def density_kernel(
    sizes, three, occupied_in, virtual_in, pairs_in, out,
    occupied, virtual, pairs, mine, table, pick, rows_in, a_msg, b_msg, a_in, b_in, b_sib, coulomb, up_out, up_in, down_out, down_in, amp,
    high, low, left, sums, dens_a, y_up, y_down, part, z_in, dens_b, w_up, w_down, v_in,
    own_sem, half_send, half_recv, t_send, t_recv, a_send, a_recv, b_send, b_recv, s_send, s_recv,
    ring_send, ring_recv, x_send, x_recv, c_send, c_recv, y_send, y_recv, z_send, z_recv, w_send, w_recv, v_send, v_recv,
):
    half, width, slab, side = sizes
    x, y, z, core = position()
    occ, aux = lax.axis_index("occ"), lax.axis_index("aux")
    me = x * NY + y
    sibling = device(x, y, z, 1 - core)
    above, below = device(x, y, lax.rem(z + 1, NZ), core), device(x, y, lax.rem(z + NZ - 1, NZ), core)
    block_rows = rows_in.shape[1]
    orbitals = block_rows // ROWS

    def occ_peer(k):
        return (lax.rem(occ + k, PAIRS), aux)

    def z_peer(k):
        return device(x, y, lax.rem(z + k, NZ), core)

    def at_offset(k, sign):
        step = lax.rem(k * 7, PLANE)
        major, minor = lax.div(step, 4), lax.rem(step, 4)
        dx = major * (1 - core) + minor * core
        dy = minor * (1 - core) + major * core
        return lax.rem(x + NX + sign * dx, NX), lax.rem(y + NY + sign * dy, NY)

    def slot(k, sign):
        to_x, to_y = at_offset(k, sign)
        return to_x * NY + to_y

    def peer(k):
        to_x, to_y = at_offset(k, 1)
        return device(to_x, to_y, z, core)

    rest = block_rows // 2

    def places(which):
        return rows_in.at[2 * which], rows_in.at[1, pl.ds(pl.multiple_of(which * rest, rest), rest)]

    def columns_of(which):
        return pl.ds(pl.multiple_of(which * half, LANES), half)

    here = places(core)
    own = [
        pltpu.make_async_copy(three.at[:block_rows, columns_of(core)], here[0], own_sem.at[0]),
        pltpu.make_async_copy(three.at[block_rows:, columns_of(core)], here[1], own_sem.at[1]),
    ]
    small = [
        pltpu.make_async_copy(pairs_in, pairs, own_sem.at[2]),
        pltpu.make_async_copy(virtual_in, virtual.at[0], own_sem.at[3]),
        pltpu.make_async_copy(occupied_in, occupied.at[0], own_sem.at[4]),
    ]
    for copy in small + own:
        copy.start()
    mine[...] = jnp.zeros_like(mine)

    barrier = pltpu.get_barrier_semaphore()
    loop(1, PAIRS, lambda k: pl.semaphore_signal(barrier, inc=1, device_id=occ_peer(k), device_id_type=MESH))
    loop(1, PLANE, lambda k: pl.semaphore_signal(barrier, inc=1, device_id=peer(k), device_id_type=MESH))
    loop(1, NZ, lambda k: pl.semaphore_signal(barrier, inc=1, device_id=z_peer(k), device_id_type=MESH))
    for other in (sibling,):
        pl.semaphore_signal(barrier, inc=1, device_id=other, device_id_type=MESH)
    small[0].wait()
    mine[0:1, 0:2] = pairs[...]
    pl.semaphore_wait(barrier, PAIRS - 1 + PLANE - 1 + NZ - 1 + 1)

    def row_out(k):
        return remote(mine, table.at[occ], t_send.at[k], t_recv.at[k], occ_peer(k))

    def row_in(k):
        came = lax.rem(occ + PAIRS - k, PAIRS)
        return remote(mine, table.at[came], t_send.at[k], t_recv.at[k], occ_peer(k))

    loop(1, PAIRS, lambda k: row_out(k).start())
    given = [
        remote(three.at[:block_rows, columns_of(1 - core)], here[0], half_send.at[0], half_recv.at[0], sibling),
        remote(three.at[block_rows:, columns_of(1 - core)], here[1], half_send.at[1], half_recv.at[1], sibling),
    ]
    for copy in given:
        copy.start()
    table[occ] = mine[...]

    small[1].wait()
    small[2].wait()
    lane = lax.broadcasted_iota(I32, (slab, 2 * half), 1)
    row = lax.broadcasted_iota(I32, (slab, 2 * half), 0)
    eb = []
    for q in range(2):
        first = lax.div(z, 4) * half + q * width + lax.rem(z, 4) * slab
        eb.append(jnp.sum(jnp.where(lane == row + first, virtual[...], 0.0), axis=1, keepdims=True))
    ea = [
        virtual[:, pl.ds(pl.multiple_of(core * half + q * width, LANES), width)] for q in range(2)
    ]

    loop(1, PAIRS, lambda k: row_in(k).wait_recv())
    orbital = lax.broadcasted_iota(I32, (1, occupied.shape[1]), 1)
    shift = jnp.zeros((1, 1), F32)
    for n in range(2):
        chosen = jnp.where(orbital == table[me, 0:1, n : n + 1], occupied[...], 0.0)
        shift = shift + jnp.sum(chosen, axis=1, keepdims=True)
    lane = lax.broadcasted_iota(I32, (ROWS, block_rows), 1)
    row = lax.broadcasted_iota(I32, (ROWS, block_rows), 0) * orbitals
    for n in range(2):
        for p in range(PAIRS):
            hit = lane == row + table[p, 0:1, n : n + 1]
            pick[n, p * ROWS : (p + 1) * ROWS, :] = jnp.where(hit, 1.0, 0.0).astype(BF16)
    for copy in own:
        copy.wait()
    for copy in given:
        copy.wait_recv()

    def plane_out(msg, into, send, recv, q, k):
        return remote(
            msg.at[q, slot(k, 1)], into.at[q, me], send.at[q, k], recv.at[q, k], peer(k)
        )

    def plane_in(msg, into, send, recv, q, k):
        came = slot(k, -1)
        return remote(msg.at[q, came], into.at[q, came], send.at[q, k], recv.at[q, k], peer(k))

    a_refs, b_refs = (a_msg, a_in, a_send, a_recv), (b_msg, b_in, b_send, b_recv)

    def pick_rows(n, msg):
        for g in range(3):
            value = jnp.dot(pick[n], rows_in[g], preferred_element_type=F32).astype(BF16)
            for q in range(2):
                msg[q, :, g * ROWS : (g + 1) * ROWS, :] = value[:, q * width : (q + 1) * width].reshape(
                    PAIRS, ROWS, width
                )

    def send_plane(refs):
        loop(1, PLANE, lambda k: plane_out(*refs, 0, k).start())
        for q in range(2):
            refs[1][q, me] = refs[0][q, me]

    def to_sibling(q, k):
        came = slot(k, -1)
        return remote(b_in.at[q, came], b_sib.at[q, came], s_send.at[q, came], s_recv.at[q, came], sibling)

    def take_b(q):
        to_sibling(q, 0).start()

        def pass_on(k):
            plane_in(*b_refs, q, k).wait_recv()
            to_sibling(q, k).start()
            if q == 0:
                plane_out(*b_refs, 0, k).wait_send()
                plane_out(*a_refs, 1, k).start()

        loop(1, PLANE, pass_on)

    def take_a(q):
        def take(k):
            plane_in(*a_refs, q, k).wait_recv()
            if q == 0:
                plane_out(*a_refs, 0, k).wait_send()
                plane_out(*b_refs, 1, k).start()

        loop(1, PLANE, take)

    def take_sibling(q):
        loop(0, PLANE, lambda k: to_sibling(q, k).wait_recv())

    pick_rows(1, b_msg)
    send_plane(b_refs)
    pick_rows(0, a_msg)
    send_plane(a_refs)

    chunks = [(0, 0), (0, 1), (1, 0), (1, 1)]

    def multiply(n, sources=(0, 1)):
        q, r = chunks[n]
        right = a_in[r].reshape(-1, width)
        for i in sources:
            source, which = ((b_in, core), (b_sib, 1 - core))[i]
            part_rows = pl.ds(pl.multiple_of(which * width, width), width)
            coulomb[n, part_rows, :] = dot_rows(source[q].reshape(-1, width), right)

    def block(n, w):
        return coulomb[n, pl.ds(pl.multiple_of(w * slab, slab), slab), :]

    mid = slab // 2
    short = coded_rows(mid, width)
    ways = ((0, up_out, up_in, above), (1, down_out, down_in, below))

    def hop(n, way, t):
        _, box, into, to = ways[way]
        slot = (n, t, slice(0, short)) if t == 0 else (n, t)
        return remote(box.at[slot], into.at[slot], ring_send.at[n, way, t], ring_recv.at[n, way, t], to)

    def ring(n, t):
        for way, box, into, _ in ways:
            w = lax.rem(z + 4 + t, NZ) if way else lax.rem(z + 4 - t, NZ)
            value = block(n, w)
            if t == 0:
                encode(value[mid:] if way else value[:mid], box.at[n, 0, :short])
            else:
                hop(n, way, t - 1).wait_recv()
                if t == 1:
                    came = decode(into.at[n, 0, :short], mid)
                    halves = [value[:mid], value[mid:]]
                    halves[way] = halves[way] + came
                    value = jnp.concatenate(halves, axis=0)
                else:
                    value = value + decode(into.at[n, t - 1], slab)
                encode(value, box.at[n, t])
            hop(n, way, t).start()

    x_next, x_prev, x_far = lax.rem(x + 1, NX), lax.rem(x + NX - 1, NX), lax.rem(x + 2, NX)
    lines = (x_next, x_prev, x_far)

    def line_out(n, i):
        q, r = chunks[n]
        ref = amp.at[core, r, x, q]
        return remote(ref, ref, x_send.at[n, i], x_recv.at[n, i], device(lines[i], y, z, core))

    def line_in(n, i):
        q, r = chunks[n]
        ref = amp.at[core, r, (x_prev, x_next, x_far)[i], q]
        return remote(ref, ref, x_send.at[n, i], x_recv.at[n, i], device(lines[i], y, z, core))

    def cross(n, i, which):
        q, r = chunks[n]
        ref = amp.at[which, r, (x_prev, x_next, x_far, x)[i], q]
        return remote(ref, ref, c_send.at[n, i], c_recv.at[n, i], sibling)

    def amplitude(n):
        q, r = chunks[n]
        hop(n, 0, STEPS - 1).wait_recv()
        hop(n, 1, STEPS - 1).wait_recv()
        total = block(n, z) + decode(up_in.at[n, STEPS - 1], slab) + decode(down_in.at[n, STEPS - 1], slab)
        encode(-total / (eb[q] + ea[r] - shift), amp.at[core, r, x, q])
        for i in range(3):
            line_out(n, i).start()
        cross(n, 3, core).start()

    def forward(n):
        for i in range(3):
            line_in(n, i).wait_recv()
            cross(n, i, core).start()

    turn = x * 2 + core
    turn_chunk, turn_shift = lax.div(turn, 4), lax.rem(width - side * lax.rem(turn, 4), width)

    def unpack(n):
        q, r = chunks[n]
        for i in range(4):
            cross(n, i, 1 - core).wait_recv()
        for h in range(2):
            for k in range(NX):
                value = decode(amp.at[h, r, k, q], slab)
                rows = slice((q * NX + k) * slab, (q * NX + k + 1) * slab)
                columns = slice(h * half + r * width, h * half + (r + 1) * width)
                top = value.astype(BF16)
                high[rows, columns] = top
                low[rows, columns] = (value - top.astype(F32)).astype(BF16)

    wide = dens_a.shape[3]
    cut = upper_rows(side)

    def turn_rows(q):
        for h in range(2):
            for k in range(NX):
                rows = slice((q * NX + k) * slab, (q * NX + k + 1) * slab)
                turned = pltpu.roll(decode(amp.at[h, turn_chunk, k, q], slab), turn_shift, 1)[:, 0:LANES]
                top = turned.astype(BF16)
                left[rows, 2 * h * LANES : (2 * h + 1) * LANES] = top
                left[rows, (2 * h + 1) * LANES : (2 * h + 2) * LANES] = (turned - top.astype(F32)).astype(BF16)

    y_next, y_prev, y_far = lax.rem(y + 1, NY), lax.rem(y + NY - 1, NY), lax.rem(y + 2, NY)
    north, south = device(x, y_next, z, core), device(x, y_prev, z, core)
    up_y = [
        remote(dens_a.at[w, h], y_up.at[i], y_send.at[i], y_recv.at[i], north)
        for i, (w, h) in enumerate(((y_far, 0), (y_next, 1), (y_next, 0)))
    ]
    down_y = [
        remote(dens_a.at[w, h], y_down.at[i], y_send.at[3 + i], y_recv.at[3 + i], south)
        for i, (w, h) in enumerate(((y_far, 1), (y_prev, 0), (y_prev, 1)))
    ]

    def product(q):
        rows = slice(q * NX * slab, (q + 1) * NX * slab)
        last = ((y_far, (up_y[0], down_y[0])), (y_next, up_y[1:2]), (y_prev, down_y[1:2]), (y, ()))
        for n, ready in last if q else [(n, ()) for n in range(NY)]:
            columns = pl.ds(pl.multiple_of(n * wide, LANES), wide)
            by_high = dot_rows(left[rows, :], high[rows, columns])
            by_low = dot_rows(left[rows, :], low[rows, columns])
            for h in range(2):
                first, second = 2 * h * LANES, (2 * h + 1) * LANES
                total = by_low[second : second + side] + by_low[first : first + side]
                total = total + by_high[second : second + side] + by_high[first : first + side]
                if q == 0:
                    sums[n, h] = total
                    continue
                total = total + sums[n, h]
                dens_a[n, h] = total[0:cut, :]
                for i in range(4):
                    dens_b[h * 4 + i, n] = column_block(total[cut:side, :], i)
            for copy in ready:
                copy.start()

    def column_block(rows, i):
        return (pltpu.roll(rows, wide - i * side, 1) if i else rows)[:, 0:LANES]

    take_b(0)
    take_a(0)
    take_sibling(0)
    multiply(0)
    ring(0, 0)
    ring(0, 1)
    take_a(1)
    multiply(1)
    ring(1, 0)
    ring(0, 2)
    ring(1, 1)
    ring(0, 3)
    take_b(1)
    multiply(2, (0,))
    ring(1, 2)
    multiply(3, (0,))
    take_sibling(1)
    multiply(2, (1,))
    ring(2, 0)
    multiply(3, (1,))
    ring(3, 0)
    amplitude(0)
    ring(1, 3)
    ring(2, 1)
    ring(3, 1)
    forward(0)
    amplitude(1)
    ring(2, 2)
    ring(3, 2)
    unpack(0)
    ring(2, 3)
    forward(1)
    ring(3, 3)
    amplitude(2)
    amplitude(3)
    unpack(1)
    turn_rows(0)
    forward(2)
    product(0)
    forward(3)
    unpack(2)
    unpack(3)
    turn_rows(1)
    product(1)

    def z_hop(rows, boxes, sems, way, t):
        into, to = boxes[way], (above, below)[way]
        w = lax.rem(z + 4 + t, NZ) if way else lax.rem(z + 4 - t, NZ)
        part_of = rows.shape[1] // 2
        some = (pl.ds(part_of, part_of) if way else pl.ds(0, part_of)) if t == 0 else slice(None)
        return remote(
            rows.at[w, some], into.at[t, some], sems[0].at[4 * way + t], sems[1].at[4 * way + t], to
        )

    def z_step(rows, boxes, sems, t):
        part_of = rows.shape[1] // 2
        for way in range(2):
            w = lax.rem(z + 4 + t, NZ) if way else lax.rem(z + 4 - t, NZ)
            if t > 0:
                z_hop(rows, boxes, sems, way, t - 1).wait_recv()
                some = (slice(part_of, None) if way else slice(0, part_of)) if t == 1 else slice(None)
                rows[w, some] = rows[w, some] + boxes[way][t - 1, some]
            z_hop(rows, boxes, sems, way, t).start()

    def z_last(rows, boxes, sems):
        z_hop(rows, boxes, sems, 0, STEPS - 1).wait_recv()
        z_hop(rows, boxes, sems, 1, STEPS - 1).wait_recv()
        return rows[z] + boxes[0][STEPS - 1] + boxes[1][STEPS - 1]

    over_b = (dens_b, (w_up, w_down), (w_send, w_recv))
    def line(k):
        return remote(part.at[lax.rem(z + k, NZ)], z_in.at[k], z_send.at[k], z_recv.at[k], z_peer(k))

    z_step(*over_b, 0)
    up_y[0].wait_recv()
    dens_a[y_next, 0] = dens_a[y_next, 0] + y_up[0]
    up_y[2].start()
    down_y[0].wait_recv()
    dens_a[y_prev, 1] = dens_a[y_prev, 1] + y_down[0]
    down_y[2].start()
    z_step(*over_b, 1)
    z_step(*over_b, 2)
    for copy in up_y[1:] + down_y[1:]:
        copy.wait_recv()
    for h, came in ((0, y_up[2] + y_down[1]), (1, y_up[1] + y_down[2])):
        total = dens_a[y, h] + came
        for i in range(4):
            part[h * 4 + i] = column_block(total, i)
    for k in (4, 3, 5, 2, 6, 1, 7):
        line(k).start()
    z_step(*over_b, 3)
    summed = z_last(*over_b)
    for n in range(NY):
        v_in[0, n] = summed[n]

    def column(i):
        w = (y_next, y_prev, y_far)[i]
        return remote(v_in.at[0, w], v_in.at[1 + i, 0], v_send.at[i], v_recv.at[i], device(x, w, z, core))

    for i in range(3):
        column(i).start()
    total = part[z]
    for k in (1, 7, 2, 6, 3, 5, 4):
        line(k).wait_recv()
        total = total + z_in[k]
    out[:cut, :] = total[:, 0:side]
    for i in range(3):
        column(i).wait_recv()
    out[cut:, :] = (v_in[0, y] + v_in[1, 0] + v_in[2, 0] + v_in[3, 0])[:, 0:side]

    for copy in given + up_y + down_y:
        copy.wait_send()
    for way in range(2):
        for t in range(STEPS):
            z_hop(*over_b, way, t).wait_send()
    for k in range(1, NZ):
        line(k).wait_send()
    for i in range(3):
        column(i).wait_send()
    loop(1, PAIRS, lambda k: row_out(k).wait_send())
    loop(1, PLANE, lambda k: plane_out(*b_refs, 1, k).wait_send())
    loop(1, PLANE, lambda k: plane_out(*a_refs, 1, k).wait_send())
    for q in range(2):
        loop(0, PLANE, lambda k, q=q: to_sibling(q, k).wait_send())
    for n in range(4):
        for way in range(2):
            for t in range(STEPS):
                hop(n, way, t).wait_send()
        for i in range(3):
            line_out(n, i).wait_send()
        for i in range(4):
            cross(n, i, core).wait_send()


def shards(three_index, occupied_energy, virtual_energy, pair_list):
    depth, orbitals, virtual = three_index.shape
    half = virtual // 2
    width = half // 2
    slab = width * 2 // NZ
    side = virtual // 16
    block_rows = ROWS * orbitals
    coded = coded_rows(slab, width)
    dma, vmem = pltpu.SemaphoreType.DMA, pltpu.VMEM
    inside = pl.BlockSpec(memory_space=vmem)
    message = (2, PLANE, 2 * depth, width)
    ring_box = (4, STEPS, coded, LANES)
    cut = upper_rows(side)
    scratch = [
        vmem((1, orbitals), F32),
        vmem((1, virtual), F32),
        vmem((1, 2), I32),
        vmem((8, LANES), I32),
        vmem((PAIRS, 8, LANES), I32),
        vmem((2, PAIRS * ROWS, block_rows), BF16),
        vmem((3, block_rows, half), BF16),
        *[vmem(message, BF16)] * 5,
        vmem((4, 2 * width, width), F32),
        *[vmem(ring_box, I16)] * 4,
        vmem((2, 2, NX, 2, coded, LANES), I16),
        *[vmem((NX * 2 * slab, virtual), BF16)] * 2,
        vmem((NX * 2 * slab, 4 * LANES), BF16),
        vmem((NY, 2, side, virtual // NY), F32),
        vmem((NY, 2, cut, virtual // NY), F32),
        *[vmem((3, cut, virtual // NY), F32)] * 2,
        vmem((NZ, cut, LANES), F32),
        vmem((NZ, cut, LANES), F32),
        vmem((NZ, NY, side - cut, LANES), F32),
        *[vmem((STEPS, NY, side - cut, LANES), F32)] * 2,
        vmem((4, NY, side - cut, LANES), F32),
        dma((5,)),
        *[dma((2,))] * 2,
        *[dma((PAIRS,))] * 2,
        *[dma((2, PLANE))] * 6,
        *[dma((4, 2, STEPS))] * 2,
        *[dma((4, 3))] * 2,
        *[dma((4, 4))] * 2,
        *[dma((6,))] * 2,
        *[dma((8,))] * 4,
        *[dma((3,))] * 2,
    ]
    return pl.pallas_call(
        functools.partial(density_kernel, (half, width, slab, side)),
        out_shape=jax.ShapeDtypeStruct((side, side), F32),
        in_specs=[pl.BlockSpec(memory_space=pltpu.HBM)] * 4,
        out_specs=inside,
        scratch_shapes=scratch,
        compiler_params=pltpu.CompilerParams(
            collective_id=0, has_side_effects=True, vmem_limit_bytes=62 * 1024 * 1024
        ),
        name="density",
    )(
        three_index.reshape(depth * orbitals, virtual),
        occupied_energy,
        virtual_energy,
        pair_list,
    )


def solution(mesh):
    placed = (P(("occ", "aux"), None, None), P(), P(), P("occ", None))
    return jax.shard_map(shards, mesh=mesh, in_specs=placed, out_specs=P("aux", "occ"), check_vma=False)
```

```python
import functools

import jax
import jax.numpy as jnp
from jax import lax
from jax.experimental import pallas as pl
from jax.experimental.pallas import tpu as pltpu
from jax.sharding import PartitionSpec as P

MESH = pl.DeviceIdType.MESH
F32 = jnp.float32
BF16 = jnp.bfloat16
I16 = jnp.int16
I32 = jnp.int32
NX, NY, NZ = 4, 4, 8
PLANE = NX * NY
PAIRS = 16
ROWS = 16
LANES = 128
STEPS = NZ // 2


def position():
    occ, aux = lax.axis_index("occ"), lax.axis_index("aux")
    core = lax.rem(aux, 2)
    x = lax.rem(lax.div(aux, 2), NX)
    z = lax.div(aux, 2 * NX) * 4 + lax.rem(occ, 4)
    return x, lax.div(occ, 4), z, core


def device(x, y, z, core):
    return (y * 4 + lax.rem(z, 4), (lax.div(z, 4) * NX + x) * 2 + core)


def remote(src, dst, send, recv, dev):
    return pltpu.make_async_remote_copy(
        src_ref=src, dst_ref=dst, send_sem=send, recv_sem=recv, device_id=dev, device_id_type=MESH
    )


def loop(first, last, body):
    def step(k, carry):
        body(k)
        return carry

    lax.fori_loop(first, last, step, 0)


def upper_rows(side):
    return side * 7 // 12 // 8 * 8


def dot_rows(a, b):
    return lax.dot_general(a, b, (((0,), (0,)), ((), ())), preferred_element_type=F32)


def coded_rows(rows, columns):
    return rows * (columns // LANES) + ROWS


def encode(block, ref):
    rows, columns = block.shape
    groups = columns // LANES
    top = jnp.maximum(jnp.max(jnp.abs(block), axis=0, keepdims=True), 1e-30)
    level = jnp.ceil(jnp.log(top) * 64.0)
    codes = jnp.round(block * (32000.0 * jnp.exp(level * (-1.0 / 64.0)))).astype(I32).astype(I16)
    row = lax.broadcasted_iota(I32, (ROWS, LANES), 0)
    tail = jnp.zeros((ROWS, LANES), F32)
    for g in range(groups):
        ref[g * rows : (g + 1) * rows, :] = codes[:, g * LANES : (g + 1) * LANES]
        tail = jnp.where(row == g, level[:, g * LANES : (g + 1) * LANES], tail)
    ref[groups * rows : groups * rows + ROWS, :] = tail.astype(I32).astype(I16)


def decode(ref, rows):
    groups = (ref.shape[0] - ROWS) // rows
    tail = ref[groups * rows : groups * rows + ROWS, :].astype(I32).astype(F32)
    scale = jnp.exp(tail * (1.0 / 64.0)) * (1.0 / 32000.0)
    parts = [
        ref[g * rows : (g + 1) * rows, :].astype(I32).astype(F32) * scale[g : g + 1, :] for g in range(groups)
    ]
    return jnp.concatenate(parts, axis=1)


def density_kernel(
    sizes, three, occupied_in, virtual_in, pairs_in, out,
    occupied, virtual, pairs, mine, table, pick, rows_in, a_msg, b_msg, a_in, b_in, b_sib, coulomb, up_out, up_in, down_out, down_in, amp,
    high, low, left, sums, dens_a, y_up, y_down, part, z_in, dens_b, w_up, w_down, v_in,
    own_sem, half_send, half_recv, t_send, t_recv, a_send, a_recv, b_send, b_recv, s_send, s_recv,
    ring_send, ring_recv, x_send, x_recv, c_send, c_recv, y_send, y_recv, z_send, z_recv, w_send, w_recv, v_send, v_recv,
):
    half, width, slab, side = sizes
    x, y, z, core = position()
    occ, aux = lax.axis_index("occ"), lax.axis_index("aux")
    me = x * NY + y
    sibling = device(x, y, z, 1 - core)
    above, below = device(x, y, lax.rem(z + 1, NZ), core), device(x, y, lax.rem(z + NZ - 1, NZ), core)
    block_rows = rows_in.shape[1]
    orbitals = block_rows // ROWS

    def occ_peer(k):
        return (lax.rem(occ + k, PAIRS), aux)

    def z_peer(k):
        return device(x, y, lax.rem(z + k, NZ), core)

    def at_offset(k, sign):
        step = lax.rem(k * 7, PLANE)
        major, minor = lax.div(step, 4), lax.rem(step, 4)
        dx = major * (1 - core) + minor * core
        dy = minor * (1 - core) + major * core
        return lax.rem(x + NX + sign * dx, NX), lax.rem(y + NY + sign * dy, NY)

    def slot(k, sign):
        to_x, to_y = at_offset(k, sign)
        return to_x * NY + to_y

    def peer(k):
        to_x, to_y = at_offset(k, 1)
        return device(to_x, to_y, z, core)

    rest = block_rows // 2

    def places(which):
        return rows_in.at[2 * which], rows_in.at[1, pl.ds(pl.multiple_of(which * rest, rest), rest)]

    def columns_of(which):
        return pl.ds(pl.multiple_of(which * half, LANES), half)

    here = places(core)
    own = [
        pltpu.make_async_copy(three.at[:block_rows, columns_of(core)], here[0], own_sem.at[0]),
        pltpu.make_async_copy(three.at[block_rows:, columns_of(core)], here[1], own_sem.at[1]),
    ]
    small = [
        pltpu.make_async_copy(pairs_in, pairs, own_sem.at[2]),
        pltpu.make_async_copy(virtual_in, virtual.at[0], own_sem.at[3]),
        pltpu.make_async_copy(occupied_in, occupied.at[0], own_sem.at[4]),
    ]
    for copy in small + own:
        copy.start()
    mine[...] = jnp.zeros_like(mine)

    barrier = pltpu.get_barrier_semaphore()
    loop(1, PAIRS, lambda k: pl.semaphore_signal(barrier, inc=1, device_id=occ_peer(k), device_id_type=MESH))
    loop(1, PLANE, lambda k: pl.semaphore_signal(barrier, inc=1, device_id=peer(k), device_id_type=MESH))
    loop(1, NZ, lambda k: pl.semaphore_signal(barrier, inc=1, device_id=z_peer(k), device_id_type=MESH))
    for other in (sibling,):
        pl.semaphore_signal(barrier, inc=1, device_id=other, device_id_type=MESH)
    small[0].wait()
    mine[0:1, 0:2] = pairs[...]
    pl.semaphore_wait(barrier, PAIRS - 1 + PLANE - 1 + NZ - 1 + 1)

    def row_out(k):
        return remote(mine, table.at[occ], t_send.at[k], t_recv.at[k], occ_peer(k))

    def row_in(k):
        came = lax.rem(occ + PAIRS - k, PAIRS)
        return remote(mine, table.at[came], t_send.at[k], t_recv.at[k], occ_peer(k))

    loop(1, PAIRS, lambda k: row_out(k).start())
    given = [
        remote(three.at[:block_rows, columns_of(1 - core)], here[0], half_send.at[0], half_recv.at[0], sibling),
        remote(three.at[block_rows:, columns_of(1 - core)], here[1], half_send.at[1], half_recv.at[1], sibling),
    ]
    for copy in given:
        copy.start()
    table[occ] = mine[...]

    small[1].wait()
    small[2].wait()
    lane = lax.broadcasted_iota(I32, (slab, 2 * half), 1)
    row = lax.broadcasted_iota(I32, (slab, 2 * half), 0)
    eb = []
    for q in range(2):
        first = lax.div(z, 4) * half + q * width + lax.rem(z, 4) * slab
        eb.append(jnp.sum(jnp.where(lane == row + first, virtual[...], 0.0), axis=1, keepdims=True))
    ea = [
        virtual[:, pl.ds(pl.multiple_of(core * half + q * width, LANES), width)] for q in range(2)
    ]

    loop(1, PAIRS, lambda k: row_in(k).wait_recv())
    orbital = lax.broadcasted_iota(I32, (1, occupied.shape[1]), 1)
    shift = jnp.zeros((1, 1), F32)
    for n in range(2):
        chosen = jnp.where(orbital == table[me, 0:1, n : n + 1], occupied[...], 0.0)
        shift = shift + jnp.sum(chosen, axis=1, keepdims=True)
    lane = lax.broadcasted_iota(I32, (ROWS, block_rows), 1)
    row = lax.broadcasted_iota(I32, (ROWS, block_rows), 0) * orbitals
    for n in range(2):
        for p in range(PAIRS):
            hit = lane == row + table[p, 0:1, n : n + 1]
            pick[n, p * ROWS : (p + 1) * ROWS, :] = jnp.where(hit, 1.0, 0.0).astype(BF16)
    for copy in own:
        copy.wait()
    for copy in given:
        copy.wait_recv()

    def plane_out(msg, into, send, recv, q, k):
        return remote(
            msg.at[q, slot(k, 1)], into.at[q, me], send.at[q, k], recv.at[q, k], peer(k)
        )

    def plane_in(msg, into, send, recv, q, k):
        came = slot(k, -1)
        return remote(msg.at[q, came], into.at[q, came], send.at[q, k], recv.at[q, k], peer(k))

    a_refs, b_refs = (a_msg, a_in, a_send, a_recv), (b_msg, b_in, b_send, b_recv)

    def pick_rows(n, msg):
        for g in range(3):
            value = jnp.dot(pick[n], rows_in[g], preferred_element_type=F32).astype(BF16)
            for q in range(2):
                msg[q, :, g * ROWS : (g + 1) * ROWS, :] = value[:, q * width : (q + 1) * width].reshape(
                    PAIRS, ROWS, width
                )

    def send_plane(refs):
        loop(1, PLANE, lambda k: plane_out(*refs, 0, k).start())
        for q in range(2):
            refs[1][q, me] = refs[0][q, me]

    def to_sibling(q, k):
        came = slot(k, -1)
        return remote(b_in.at[q, came], b_sib.at[q, came], s_send.at[q, came], s_recv.at[q, came], sibling)

    def take_b(q):
        to_sibling(q, 0).start()

        def pass_on(k):
            plane_in(*b_refs, q, k).wait_recv()
            to_sibling(q, k).start()
            if q == 0:
                plane_out(*b_refs, 0, k).wait_send()
                plane_out(*a_refs, 1, k).start()

        loop(1, PLANE, pass_on)

    def take_a(q):
        def take(k):
            plane_in(*a_refs, q, k).wait_recv()
            if q == 0:
                plane_out(*a_refs, 0, k).wait_send()
                plane_out(*b_refs, 1, k).start()

        loop(1, PLANE, take)

    def take_sibling(q):
        loop(0, PLANE, lambda k: to_sibling(q, k).wait_recv())

    pick_rows(1, b_msg)
    send_plane(b_refs)
    pick_rows(0, a_msg)
    send_plane(a_refs)

    chunks = [(0, 0), (0, 1), (1, 0), (1, 1)]

    def multiply(n, sources=(0, 1)):
        q, r = chunks[n]
        right = a_in[r].reshape(-1, width)
        for i in sources:
            source, which = ((b_in, core), (b_sib, 1 - core))[i]
            part_rows = pl.ds(pl.multiple_of(which * width, width), width)
            coulomb[n, part_rows, :] = dot_rows(source[q].reshape(-1, width), right)

    def block(n, w):
        return coulomb[n, pl.ds(pl.multiple_of(w * slab, slab), slab), :]

    mid = slab // 2
    short = coded_rows(mid, width)
    ways = ((0, up_out, up_in, above), (1, down_out, down_in, below))

    def hop(n, way, t):
        _, box, into, to = ways[way]
        slot = (n, t, slice(0, short)) if t == 0 else (n, t)
        return remote(box.at[slot], into.at[slot], ring_send.at[n, way, t], ring_recv.at[n, way, t], to)

    def ring(n, t):
        for way, box, into, _ in ways:
            w = lax.rem(z + 4 + t, NZ) if way else lax.rem(z + 4 - t, NZ)
            value = block(n, w)
            if t == 0:
                encode(value[mid:] if way else value[:mid], box.at[n, 0, :short])
            else:
                hop(n, way, t - 1).wait_recv()
                if t == 1:
                    came = decode(into.at[n, 0, :short], mid)
                    halves = [value[:mid], value[mid:]]
                    halves[way] = halves[way] + came
                    value = jnp.concatenate(halves, axis=0)
                else:
                    value = value + decode(into.at[n, t - 1], slab)
                encode(value, box.at[n, t])
            hop(n, way, t).start()

    x_next, x_prev, x_far = lax.rem(x + 1, NX), lax.rem(x + NX - 1, NX), lax.rem(x + 2, NX)
    lines = (x_next, x_prev, x_far)

    def line_out(n, i):
        q, r = chunks[n]
        ref = amp.at[core, r, x, q]
        return remote(ref, ref, x_send.at[n, i], x_recv.at[n, i], device(lines[i], y, z, core))

    def line_in(n, i):
        q, r = chunks[n]
        ref = amp.at[core, r, (x_prev, x_next, x_far)[i], q]
        return remote(ref, ref, x_send.at[n, i], x_recv.at[n, i], device(lines[i], y, z, core))

    def cross(n, i, which):
        q, r = chunks[n]
        ref = amp.at[which, r, (x_prev, x_next, x_far, x)[i], q]
        return remote(ref, ref, c_send.at[n, i], c_recv.at[n, i], sibling)

    def amplitude(n):
        q, r = chunks[n]
        hop(n, 0, STEPS - 1).wait_recv()
        hop(n, 1, STEPS - 1).wait_recv()
        total = block(n, z) + decode(up_in.at[n, STEPS - 1], slab) + decode(down_in.at[n, STEPS - 1], slab)
        encode(-total / (eb[q] + ea[r] - shift), amp.at[core, r, x, q])
        for i in range(3):
            line_out(n, i).start()
        cross(n, 3, core).start()

    def forward(n):
        for i in range(3):
            line_in(n, i).wait_recv()
            cross(n, i, core).start()

    turn = x * 2 + core
    turn_chunk, turn_shift = lax.div(turn, 4), lax.rem(width - side * lax.rem(turn, 4), width)

    def unpack(n):
        q, r = chunks[n]
        for i in range(4):
            cross(n, i, 1 - core).wait_recv()
        for h in range(2):
            for k in range(NX):
                value = decode(amp.at[h, r, k, q], slab)
                rows = slice((q * NX + k) * slab, (q * NX + k + 1) * slab)
                columns = slice(h * half + r * width, h * half + (r + 1) * width)
                top = value.astype(BF16)
                high[rows, columns] = top
                low[rows, columns] = (value - top.astype(F32)).astype(BF16)

    wide = dens_a.shape[3]
    cut = upper_rows(side)

    def turn_rows(q):
        for h in range(2):
            for k in range(NX):
                rows = slice((q * NX + k) * slab, (q * NX + k + 1) * slab)
                turned = pltpu.roll(decode(amp.at[h, turn_chunk, k, q], slab), turn_shift, 1)[:, 0:LANES]
                top = turned.astype(BF16)
                left[rows, 2 * h * LANES : (2 * h + 1) * LANES] = top
                left[rows, (2 * h + 1) * LANES : (2 * h + 2) * LANES] = (turned - top.astype(F32)).astype(BF16)

    y_next, y_prev, y_far = lax.rem(y + 1, NY), lax.rem(y + NY - 1, NY), lax.rem(y + 2, NY)
    north, south = device(x, y_next, z, core), device(x, y_prev, z, core)
    up_y = [
        remote(dens_a.at[w, h], y_up.at[i], y_send.at[i], y_recv.at[i], north)
        for i, (w, h) in enumerate(((y_far, 0), (y_next, 1), (y_next, 0)))
    ]
    down_y = [
        remote(dens_a.at[w, h], y_down.at[i], y_send.at[3 + i], y_recv.at[3 + i], south)
        for i, (w, h) in enumerate(((y_far, 1), (y_prev, 0), (y_prev, 1)))
    ]

    def product(q):
        rows = slice(q * NX * slab, (q + 1) * NX * slab)
        last = ((y_far, (up_y[0], down_y[0])), (y_next, up_y[1:2]), (y_prev, down_y[1:2]), (y, ()))
        for n, ready in last if q else [(n, ()) for n in range(NY)]:
            columns = pl.ds(pl.multiple_of(n * wide, LANES), wide)
            by_high = dot_rows(left[rows, :], high[rows, columns])
            by_low = dot_rows(left[rows, :], low[rows, columns])
            for h in range(2):
                first, second = 2 * h * LANES, (2 * h + 1) * LANES
                total = by_low[second : second + side] + by_low[first : first + side]
                total = total + by_high[second : second + side] + by_high[first : first + side]
                if q == 0:
                    sums[n, h] = total
                    continue
                total = total + sums[n, h]
                dens_a[n, h] = total[0:cut, :]
                for i in range(4):
                    dens_b[h * 4 + i, n] = column_block(total[cut:side, :], i)
            for copy in ready:
                copy.start()

    def column_block(rows, i):
        return (pltpu.roll(rows, wide - i * side, 1) if i else rows)[:, 0:LANES]

    take_b(0)
    take_a(0)
    take_sibling(0)
    multiply(0)
    ring(0, 0)
    ring(0, 1)
    take_a(1)
    multiply(1)
    ring(1, 0)
    ring(0, 2)
    ring(1, 1)
    ring(0, 3)
    take_b(1)
    multiply(2, (0,))
    ring(1, 2)
    multiply(3, (0,))
    take_sibling(1)
    multiply(2, (1,))
    ring(2, 0)
    multiply(3, (1,))
    ring(3, 0)
    amplitude(0)
    ring(1, 3)
    ring(2, 1)
    ring(3, 1)
    forward(0)
    amplitude(1)
    ring(2, 2)
    ring(3, 2)
    unpack(0)
    ring(2, 3)
    forward(1)
    ring(3, 3)
    amplitude(2)
    amplitude(3)
    unpack(1)
    turn_rows(0)
    forward(2)
    forward(3)
    product(0)
    unpack(2)
    unpack(3)
    turn_rows(1)
    product(1)

    def z_hop(rows, boxes, sems, way, t):
        into, to = boxes[way], (above, below)[way]
        w = lax.rem(z + 4 + t, NZ) if way else lax.rem(z + 4 - t, NZ)
        part_of = rows.shape[1] // 2
        some = (pl.ds(part_of, part_of) if way else pl.ds(0, part_of)) if t == 0 else slice(None)
        return remote(
            rows.at[w, some], into.at[t, some], sems[0].at[4 * way + t], sems[1].at[4 * way + t], to
        )

    def z_step(rows, boxes, sems, t):
        part_of = rows.shape[1] // 2
        for way in range(2):
            w = lax.rem(z + 4 + t, NZ) if way else lax.rem(z + 4 - t, NZ)
            if t > 0:
                z_hop(rows, boxes, sems, way, t - 1).wait_recv()
                some = (slice(part_of, None) if way else slice(0, part_of)) if t == 1 else slice(None)
                rows[w, some] = rows[w, some] + boxes[way][t - 1, some]
            z_hop(rows, boxes, sems, way, t).start()

    def z_last(rows, boxes, sems):
        z_hop(rows, boxes, sems, 0, STEPS - 1).wait_recv()
        z_hop(rows, boxes, sems, 1, STEPS - 1).wait_recv()
        return rows[z] + boxes[0][STEPS - 1] + boxes[1][STEPS - 1]

    over_b = (dens_b, (w_up, w_down), (w_send, w_recv))
    def line(k):
        return remote(part.at[lax.rem(z + k, NZ)], z_in.at[k], z_send.at[k], z_recv.at[k], z_peer(k))

    z_step(*over_b, 0)
    up_y[0].wait_recv()
    dens_a[y_next, 0] = dens_a[y_next, 0] + y_up[0]
    up_y[2].start()
    down_y[0].wait_recv()
    dens_a[y_prev, 1] = dens_a[y_prev, 1] + y_down[0]
    down_y[2].start()
    z_step(*over_b, 1)
    z_step(*over_b, 2)
    for copy in up_y[1:] + down_y[1:]:
        copy.wait_recv()
    for h, came in ((0, y_up[2] + y_down[1]), (1, y_up[1] + y_down[2])):
        total = dens_a[y, h] + came
        for i in range(4):
            part[h * 4 + i] = column_block(total, i)
    for k in (4, 3, 5, 2, 6, 1, 7):
        line(k).start()
    z_step(*over_b, 3)
    summed = z_last(*over_b)
    for n in range(NY):
        v_in[0, n] = summed[n]

    def column(i):
        w = (y_next, y_prev, y_far)[i]
        return remote(v_in.at[0, w], v_in.at[1 + i, 0], v_send.at[i], v_recv.at[i], device(x, w, z, core))

    for i in range(3):
        column(i).start()
    total = part[z]
    for k in (1, 7, 2, 6, 3, 5, 4):
        line(k).wait_recv()
        total = total + z_in[k]
    out[:cut, :] = total[:, 0:side]
    for i in range(3):
        column(i).wait_recv()
    out[cut:, :] = (v_in[0, y] + v_in[1, 0] + v_in[2, 0] + v_in[3, 0])[:, 0:side]

    for copy in given + up_y + down_y:
        copy.wait_send()
    for way in range(2):
        for t in range(STEPS):
            z_hop(*over_b, way, t).wait_send()
    for k in range(1, NZ):
        line(k).wait_send()
    for i in range(3):
        column(i).wait_send()
    loop(1, PAIRS, lambda k: row_out(k).wait_send())
    loop(1, PLANE, lambda k: plane_out(*b_refs, 1, k).wait_send())
    loop(1, PLANE, lambda k: plane_out(*a_refs, 1, k).wait_send())
    for q in range(2):
        loop(0, PLANE, lambda k, q=q: to_sibling(q, k).wait_send())
    for n in range(4):
        for way in range(2):
            for t in range(STEPS):
                hop(n, way, t).wait_send()
        for i in range(3):
            line_out(n, i).wait_send()
        for i in range(4):
            cross(n, i, core).wait_send()


def shards(three_index, occupied_energy, virtual_energy, pair_list):
    depth, orbitals, virtual = three_index.shape
    half = virtual // 2
    width = half // 2
    slab = width * 2 // NZ
    side = virtual // 16
    block_rows = ROWS * orbitals
    coded = coded_rows(slab, width)
    dma, vmem = pltpu.SemaphoreType.DMA, pltpu.VMEM
    inside = pl.BlockSpec(memory_space=vmem)
    message = (2, PLANE, 2 * depth, width)
    ring_box = (4, STEPS, coded, LANES)
    cut = upper_rows(side)
    scratch = [
        vmem((1, orbitals), F32),
        vmem((1, virtual), F32),
        vmem((1, 2), I32),
        vmem((8, LANES), I32),
        vmem((PAIRS, 8, LANES), I32),
        vmem((2, PAIRS * ROWS, block_rows), BF16),
        vmem((3, block_rows, half), BF16),
        *[vmem(message, BF16)] * 5,
        vmem((4, 2 * width, width), F32),
        *[vmem(ring_box, I16)] * 4,
        vmem((2, 2, NX, 2, coded, LANES), I16),
        *[vmem((NX * 2 * slab, virtual), BF16)] * 2,
        vmem((NX * 2 * slab, 4 * LANES), BF16),
        vmem((NY, 2, side, virtual // NY), F32),
        vmem((NY, 2, cut, virtual // NY), F32),
        *[vmem((3, cut, virtual // NY), F32)] * 2,
        vmem((NZ, cut, LANES), F32),
        vmem((NZ, cut, LANES), F32),
        vmem((NZ, NY, side - cut, LANES), F32),
        *[vmem((STEPS, NY, side - cut, LANES), F32)] * 2,
        vmem((4, NY, side - cut, LANES), F32),
        dma((5,)),
        *[dma((2,))] * 2,
        *[dma((PAIRS,))] * 2,
        *[dma((2, PLANE))] * 6,
        *[dma((4, 2, STEPS))] * 2,
        *[dma((4, 3))] * 2,
        *[dma((4, 4))] * 2,
        *[dma((6,))] * 2,
        *[dma((8,))] * 4,
        *[dma((3,))] * 2,
    ]
    return pl.pallas_call(
        functools.partial(density_kernel, (half, width, slab, side)),
        out_shape=jax.ShapeDtypeStruct((side, side), F32),
        in_specs=[pl.BlockSpec(memory_space=pltpu.HBM)] * 4,
        out_specs=inside,
        scratch_shapes=scratch,
        compiler_params=pltpu.CompilerParams(
            collective_id=0, has_side_effects=True, vmem_limit_bytes=62 * 1024 * 1024
        ),
        name="density",
    )(
        three_index.reshape(depth * orbitals, virtual),
        occupied_energy,
        virtual_energy,
        pair_list,
    )


def solution(mesh):
    placed = (P(("occ", "aux"), None, None), P(), P(), P("occ", None))
    return jax.shard_map(shards, mesh=mesh, in_specs=placed, out_specs=P("aux", "occ"), check_vma=False)
```
